32 devices in a mesh: grp: 2 (over y), gr: 4 (over x, core), gc: 4 (over z).
Axes of the slice: x: 2, y: 2, z: 4, core: 2. Of those that a mesh axis runs over, the one named last changes fastest.
Arguments:
- activations: bfloat16 [256, 32, 4096], P(('grp', 'gr', 'gc')), parts along dimension 0, may hold values from -6 to 6
- out_grads: bfloat16 [256, 32, 4096], P(('grp', 'gr', 'gc')), parts along dimension 0, may hold values from -6 to 6
- proj_in: bfloat16 [4096, 64], replicated, may hold values from -0.09375 to 0.09375
- proj_out: bfloat16 [4096, 64], replicated, may hold values from -0.09375 to 0.09375
- inv_gram: bfloat16 [4096, 4096], P('gr', 'gc'), may hold values from -1 to 2, as said below
Outputs:
- kernel: float32 [256, 128], P(('grp', 'gr'), 'gc'), parts along dimension 0
The draws below stay inside these ranges and needn't reach their ends.
There are 2 independent parts, one for each index of `grp`. The reference program is written for one: setup_inputs(seed, part) draws one part's arguments, and reference() takes and returns one part's arrays. A program takes and returns all parts, laid end to end along the dimension named above; an argument that names none is the same for every part. Nothing has to cross between parts.
Inputs may be any that keep to these rules, and one draw needn't show every extreme that they name: inv_gram is symmetric and positive definite.
All inputs are finite; a program needn't handle non-finite values.
Results may differ from the reference program's by a relative error of at most 0.0016.
Values may be sent and summed in bfloat16 or wider, within the bound.
No kernel may reach another device: no remote copies, remote signals or barrier semaphores. Data moves between devices by JAX's collectives and lax.ppermute only.
A program may use at most 64 MiB of HBM per device.

```python
import math
import jax
import jax.numpy as jnp
from jax import lax

D = 4096
PROJ = 64
LEN = 32
FEAT = 4096
SEQ = 128


def draw_inv_gram(key, part):
    key = jax.random.fold_in(key, 7)
    first, second = jax.random.split(key)
    base = jax.random.normal(first, (FEAT, FEAT), jnp.float32)
    offdiag = (base + base.T) * (0.2 / jnp.sqrt(jnp.float32(FEAT)))
    diagonal = jax.random.uniform(second, (FEAT,), jnp.float32, 1.0, 2.0)
    identity = jnp.eye(FEAT, dtype=jnp.float32)
    return (offdiag * (1.0 - identity) + identity * diagonal[None, :]).astype(jnp.bfloat16)


def shard_levels(own_key, dims, pieces, least, top_value):
    loudness, own = 1.0, jax.random.fold_in(own_key, 6)
    for position, blocks in pieces:
        steps = jnp.exp(jax.random.uniform(jax.random.fold_in(own, position), (blocks,), jnp.float32, least / len(pieces), top_value / len(pieces)))
        loudness = loudness * jnp.repeat(steps, dims[position] // blocks).reshape([-1 if axis == position else 1 for axis in range(len(dims))])
    return loudness


def normal_values(key, shape, deviation, most, pieces=(), held_as=jnp.bfloat16):
    drawn = jax.random.normal(key, shape, jnp.float32) * deviation
    if len(pieces) > 0:
        drawn = shard_levels(key, shape, pieces, -0.22, 0.18) * drawn
    return jnp.clip(drawn, min=-most, max=most).astype(held_as)


def setup_inputs(seed: int = 0, part: int = 0) -> dict:
    streams_of = jax.random.split(jax.random.key(seed), 6)
    part_keys = jax.random.split(jax.random.fold_in(streams_of[5], part), 6)
    return {
        "activations": normal_values(part_keys[0], (SEQ, LEN, D), 1.0, 6.0, ((0, 16),)),
        "out_grads": normal_values(part_keys[1], (SEQ, LEN, D), 1.0, 6.0, ((0, 16),)),
        "proj_in": normal_values(streams_of[2], (D, PROJ), D ** -0.5, 0.09375),
        "proj_out": normal_values(streams_of[3], (D, PROJ), D ** -0.5, 0.09375),
        "inv_gram": draw_inv_gram(jax.random.fold_in(streams_of[5], 71), part),
    }


def reference(activations, out_grads, proj_in, proj_out, inv_gram):
    seqs, length, width = activations.shape
    rank = proj_in.shape[1]
    proj_act = jnp.dot(activations.reshape(seqs * length, width), proj_in, preferred_element_type=jnp.float32).astype(jnp.bfloat16)
    proj_grad = jnp.dot(out_grads.reshape(seqs * length, width), proj_out, preferred_element_type=jnp.float32).astype(jnp.bfloat16)
    proj_act = proj_act.reshape(seqs, length, rank).astype(jnp.float32)
    proj_grad = proj_grad.reshape(seqs, length, rank).astype(jnp.float32)
    summed = jnp.einsum('sto,sti->soi', proj_grad, proj_act).reshape(seqs, rank * rank)
    grad_rows = (summed * (1.0 / math.sqrt(length))).astype(jnp.bfloat16)
    precond = jnp.dot(grad_rows, inv_gram, preferred_element_type=jnp.float32).astype(jnp.bfloat16)
    kernel = lax.dot_general(precond, grad_rows, (((1,), (1,)), ((), ())), preferred_element_type=jnp.float32)
    return kernel * (8.0 / (rank * rank))
```

```python
import math

import jax
import jax.numpy as jnp
from jax import lax
from jax.sharding import PartitionSpec as P


def per_device(rows_n, cols_n, activations, out_grads, proj_in, proj_out, inv_gram):
    seqs, length, width = activations.shape
    rank = proj_in.shape[1]
    feat = rank * rank
    row_block, col_block = inv_gram.shape
    n = rows_n * cols_n
    total = seqs * n
    proj_act = jnp.dot(
        activations.reshape(seqs * length, width), proj_in, preferred_element_type=jnp.float32
    ).astype(jnp.bfloat16)
    proj_grad = jnp.dot(
        out_grads.reshape(seqs * length, width), proj_out, preferred_element_type=jnp.float32
    ).astype(jnp.bfloat16)
    proj_act = proj_act.reshape(seqs, length, rank)
    proj_grad = proj_grad.reshape(seqs, length, rank)
    summed = jnp.einsum(
        "sto,sti->soi", proj_grad, proj_act, preferred_element_type=jnp.float32
    ).reshape(seqs, feat)
    own_rows = (summed * (1.0 / math.sqrt(length))).astype(jnp.bfloat16)

    by_row = jnp.stack([own_rows[:, r * row_block : (r + 1) * row_block] for r in range(rows_n)])
    by_col = jnp.stack([own_rows[:, c * col_block : (c + 1) * col_block] for c in range(cols_n)])
    by_row = jnp.broadcast_to(by_row[:, None], (rows_n, cols_n, seqs, row_block))
    by_col = jnp.broadcast_to(by_col[None, :], (rows_n, cols_n, seqs, col_block))
    pieces = jnp.concatenate([by_row, by_col], axis=3).reshape(n, seqs, row_block + col_block)
    got = lax.all_to_all(pieces, ("gr", "gc"), 0, 0, tiled=True)
    got = got.reshape(total, row_block + col_block)

    precond = jnp.dot(
        got[:, :row_block], inv_gram, preferred_element_type=jnp.float32
    ).astype(jnp.bfloat16)
    terms = lax.dot_general(
        precond, got[:, row_block:], (((1,), (1,)), ((), ())), preferred_element_type=jnp.float32
    ) * (8.0 / feat)
    tall, wide = total // rows_n, total // cols_n
    terms = terms.reshape(rows_n, tall, cols_n, wide).transpose(0, 2, 1, 3).reshape(n, tall, wide)
    return jnp.sum(lax.all_to_all(terms, ("gr", "gc"), 0, 0, tiled=True), axis=0)


def solution(mesh):
    in_specs = (
        P(("grp", "gr", "gc"), None, None),
        P(("grp", "gr", "gc"), None, None),
        P(),
        P(),
        P("gr", "gc"),
    )
    out_specs = P(("grp", "gr"), "gc")

    def fn(*args):
        return per_device(mesh.shape["gr"], mesh.shape["gc"], *args)

    return jax.shard_map(fn, mesh=mesh, in_specs=in_specs, out_specs=out_specs, check_vma=False)
```

```python
import math

import jax
import jax.numpy as jnp
from jax import lax
from jax.sharding import PartitionSpec as P


def back(value, axis, steps, size):
    if steps % size == 0:
        return value
    return lax.ppermute(value, axis, [(i, (i + steps) % size) for i in range(size)])


def per_device(n, activations, out_grads, proj_in, proj_out, inv_gram):
    seqs, length, width = activations.shape
    rank = proj_in.shape[1]
    feat = rank * rank
    block = inv_gram.shape[0]
    total = seqs * n * n
    tall = total // n
    row, col = lax.axis_index("gr"), lax.axis_index("gc")
    proj_act = jnp.dot(
        activations.reshape(seqs * length, width), proj_in, preferred_element_type=jnp.float32
    ).astype(jnp.bfloat16)
    proj_grad = jnp.dot(
        out_grads.reshape(seqs * length, width), proj_out, preferred_element_type=jnp.float32
    ).astype(jnp.bfloat16)
    proj_act = proj_act.reshape(seqs, length, rank)
    proj_grad = proj_grad.reshape(seqs, length, rank)
    summed = jnp.einsum(
        "sto,sti->soi", proj_grad, proj_act, preferred_element_type=jnp.float32
    ).reshape(seqs, feat)
    own_rows = (summed * (1.0 / math.sqrt(length))).astype(jnp.bfloat16)

    def features(place):
        return lax.dynamic_slice_in_dim(own_rows, lax.rem(place, n) * block, block, 1)

    def in_order(pieces):
        return lax.dynamic_slice_in_dim(jnp.stack(pieces[::-1] * 2), n - 1 - col, n)

    by_col = [back(features(col + k), "gc", k, n) for k in range(n)]
    by_row = [back(features(row + k), "gr", k, n) for k in range(n)]
    by_col = in_order(by_col).reshape(tall, block)
    by_row = jnp.concatenate(by_row)
    left = in_order([back(by_row, "gc", j, n) for j in range(n)]).reshape(total, block)
    right = [back(by_col, "gr", k, n) for k in range(n)]
    turn = lax.rem(row - col + n, n)
    right = lax.dynamic_slice_in_dim(jnp.stack(right * 2), turn, n).reshape(total, block)

    precond = jnp.dot(left, inv_gram, preferred_element_type=jnp.float32).astype(jnp.bfloat16)
    terms = lax.dot_general(
        precond, right, (((1,), (1,)), ((), ())), preferred_element_type=jnp.float32
    ) * (8.0 / feat)
    terms = terms.reshape(n, n, seqs, total).transpose(1, 0, 2, 3).reshape(n, tall, total)
    rows = terms[0]
    for k in range(1, n):
        rows = rows + back(terms[k], "gr", n - k, n)
    rows = rows.reshape(tall, n, tall)
    out = rows[:, 0]
    for m in range(1, n):
        out = out + back(rows[:, m], "gc", n - m, n)
    return out


def solution(mesh):
    in_specs = (
        P(("grp", "gr", "gc"), None, None),
        P(("grp", "gr", "gc"), None, None),
        P(),
        P(),
        P("gr", "gc"),
    )
    out_specs = P(("grp", "gr"), "gc")

    def fn(*args):
        return per_device(mesh.shape["gr"], *args)

    return jax.shard_map(fn, mesh=mesh, in_specs=in_specs, out_specs=out_specs, check_vma=False)
```

```python
import math

import jax
import jax.numpy as jnp
from jax import lax
from jax.sharding import Mesh, PartitionSpec as P

PLANE = ("chip", "gc")


def other_core(value):
    return lax.ppermute(value, "core", [(0, 1), (1, 0)])


def per_device(chips, cols, activations, out_grads, proj_in, proj_out, inv_gram):
    seqs, length, width = activations.shape
    rank = proj_in.shape[1]
    feat = rank * rank
    row_block, col_block = inv_gram.shape
    plane = chips * cols
    half = seqs * plane
    tall = half // chips
    core = lax.axis_index("core")

    inv_other = other_core(inv_gram)

    proj_act = jnp.dot(
        activations.reshape(seqs * length, width), proj_in, preferred_element_type=jnp.float32
    ).astype(jnp.bfloat16)
    proj_grad = jnp.dot(
        out_grads.reshape(seqs * length, width), proj_out, preferred_element_type=jnp.float32
    ).astype(jnp.bfloat16)
    proj_act = proj_act.reshape(seqs, length, rank)
    proj_grad = proj_grad.reshape(seqs, length, rank)
    summed = jnp.einsum(
        "sto,sti->soi", proj_grad, proj_act, preferred_element_type=jnp.float32
    ).reshape(seqs, feat)
    own_rows = (summed * (1.0 / math.sqrt(length))).astype(jnp.bfloat16)

    pieces = []
    for chip in range(chips):
        low = own_rows[:, 2 * chip * row_block : (2 * chip + 1) * row_block]
        high = own_rows[:, (2 * chip + 1) * row_block : (2 * chip + 2) * row_block]
        own, other = jnp.where(core == 0, low, high), jnp.where(core == 0, high, low)
        for col in range(cols):
            pieces.append(
                jnp.concatenate([own, other, own_rows[:, col * col_block : (col + 1) * col_block]], axis=1)
            )
    got = lax.all_to_all(jnp.stack(pieces), PLANE, 0, 0, tiled=True)
    got = got.reshape(half, 2 * row_block + col_block)

    mine = got[:, 2 * row_block :]
    theirs = other_core(mine)
    precond = jnp.dot(got[:, :row_block], inv_gram, preferred_element_type=jnp.float32)
    precond += jnp.dot(
        got[:, row_block : 2 * row_block], inv_other, preferred_element_type=jnp.float32
    )
    precond = precond.astype(jnp.bfloat16)
    mine = mine.reshape(chips, 1, tall, col_block)
    theirs = theirs.reshape(chips, 1, tall, col_block)
    right = jnp.where(
        core == 0,
        jnp.concatenate([mine, theirs], axis=1),
        jnp.concatenate([theirs, mine], axis=1),
    ).reshape(2 * half, col_block)
    terms = lax.dot_general(
        precond, right, (((1,), (1,)), ((), ())), preferred_element_type=jnp.float32
    ) * (8.0 / feat)

    wide = 2 * half // cols
    fold = max(1, 128 // wide)
    terms = terms.reshape(chips, fold, tall // fold, cols, wide).transpose(0, 3, 2, 1, 4)
    terms = terms.reshape(plane, tall // fold, fold * wide)
    total = jnp.sum(lax.all_to_all(terms, PLANE, 0, 0, tiled=True), axis=0)
    return jnp.concatenate([total[:, i * wide : (i + 1) * wide] for i in range(fold)])


def solution(mesh):
    grp, gr, gc = (mesh.shape[name] for name in ("grp", "gr", "gc"))
    split = Mesh(mesh.devices.reshape(grp, gr // 2, 2, gc), ("grp", "chip", "core", "gc"))
    rows = ("grp", "chip", "core", "gc")
    in_specs = (P(rows, None, None), P(rows, None, None), P(), P(), P(("chip", "core"), "gc"))
    out_specs = P(("grp", "chip", "core"), "gc")

    def fn(*args):
        return per_device(gr // 2, gc, *args)

    return jax.shard_map(fn, mesh=split, in_specs=in_specs, out_specs=out_specs, check_vma=False)
```

```python
import math

import jax
import jax.numpy as jnp
from jax import lax
from jax.sharding import Mesh, PartitionSpec as P

PLANE = ("chip", "gc")


def other_core(value):
    return lax.ppermute(value, "core", [(0, 1), (1, 0)])


def per_device(chips, cols, activations, out_grads, proj_in, proj_out, inv_gram):
    seqs, length, width = activations.shape
    rank = proj_in.shape[1]
    feat = rank * rank
    row_block, col_block = inv_gram.shape
    plane = chips * cols
    half = seqs * plane
    tall = half // chips
    core = lax.axis_index("core")

    inv_other = other_core(inv_gram)

    proj_act = jnp.dot(
        activations.reshape(seqs * length, width), proj_in, preferred_element_type=jnp.float32
    ).astype(jnp.bfloat16)
    proj_grad = jnp.dot(
        out_grads.reshape(seqs * length, width), proj_out, preferred_element_type=jnp.float32
    ).astype(jnp.bfloat16)
    proj_act = proj_act.reshape(seqs, length, rank)
    proj_grad = proj_grad.reshape(seqs, length, rank)
    summed = jnp.einsum(
        "sto,sti->soi", proj_grad, proj_act, preferred_element_type=jnp.float32
    ).reshape(seqs, feat)
    own_rows = (summed * (1.0 / math.sqrt(length))).astype(jnp.bfloat16)

    pieces = []
    for chip in range(chips):
        low = own_rows[:, 2 * chip * row_block : (2 * chip + 1) * row_block]
        high = own_rows[:, (2 * chip + 1) * row_block : (2 * chip + 2) * row_block]
        piece = jnp.where(
            core == 0, jnp.concatenate([low, high], axis=1), jnp.concatenate([high, low], axis=1)
        )
        pieces.extend([piece] * cols)
    got = lax.all_to_all(jnp.stack(pieces), PLANE, 0, 0, tiled=True).reshape(half, 2 * row_block)
    own, other = got[:, :row_block], got[:, row_block:]

    col = lax.axis_index("gc")
    held = jnp.where(col % 2 == core, own, other)
    own_terms = jnp.dot(own, inv_gram, preferred_element_type=jnp.float32)
    mine = held
    for step in range(1, chips):
        pairs = [
            (z // 2 * cols + z, (z // 2 + step) % chips * cols + z) for z in range(cols)
        ]
        moved, own_terms = lax.optimization_barrier((lax.ppermute(held, PLANE, pairs), own_terms))
        mine = jnp.where(lax.axis_index("chip") == (col // 2 + step) % chips, moved, mine)
    theirs = other_core(mine)
    precond = own_terms + jnp.dot(other, inv_other, preferred_element_type=jnp.float32)
    precond = precond.astype(jnp.bfloat16)
    mine = mine.reshape(chips, 1, tall, col_block)
    theirs = theirs.reshape(chips, 1, tall, col_block)
    right = jnp.where(
        core == 0,
        jnp.concatenate([mine, theirs], axis=1),
        jnp.concatenate([theirs, mine], axis=1),
    ).reshape(2 * half, col_block)
    terms = lax.dot_general(
        precond, right, (((1,), (1,)), ((), ())), preferred_element_type=jnp.float32
    ) * (8.0 / feat)

    wide = 2 * half // cols
    fold = max(1, 128 // wide)
    terms = terms.reshape(chips, fold, tall // fold, cols, wide).transpose(0, 3, 2, 1, 4)
    terms = terms.reshape(plane, tall // fold, fold * wide)
    total = jnp.sum(lax.all_to_all(terms, PLANE, 0, 0, tiled=True), axis=0)
    return jnp.concatenate([total[:, i * wide : (i + 1) * wide] for i in range(fold)])


def solution(mesh):
    grp, gr, gc = (mesh.shape[name] for name in ("grp", "gr", "gc"))
    split = Mesh(mesh.devices.reshape(grp, gr // 2, 2, gc), ("grp", "chip", "core", "gc"))
    rows = ("grp", "chip", "core", "gc")
    in_specs = (P(rows, None, None), P(rows, None, None), P(), P(), P(("chip", "core"), "gc"))
    out_specs = P(("grp", "chip", "core"), "gc")

    def fn(*args):
        return per_device(gr // 2, gc, *args)

    return jax.shard_map(fn, mesh=split, in_specs=in_specs, out_specs=out_specs, check_vma=False)
```

```python
import functools
import math

import jax
import jax.numpy as jnp
from jax import lax
from jax.experimental import pallas as pl
from jax.experimental.pallas import tpu as pltpu
from jax.sharding import Mesh, PartitionSpec as P

PLANE = ("chip", "gc")
CHUNK = 64
VMEM = pl.BlockSpec(memory_space=pltpu.VMEM)
HBM = pl.BlockSpec(memory_space=pl.ANY)
NT = (((1,), (1,)), ((), ()))


def other_core(value):
    return lax.ppermute(value, "core", [(0, 1), (1, 0)])


def project_kernel(act, grad, w_in, w_out, pa, pg, act_v, grad_v, in_v, out_v, w_sem, x_sem):
    rows = act.shape[0]
    steps = rows // CHUNK
    weights = [
        pltpu.make_async_copy(w_in, in_v, w_sem.at[0]),
        pltpu.make_async_copy(w_out, out_v, w_sem.at[1]),
    ]
    copies = []
    for side, (src, dst) in enumerate(((act, act_v), (grad, grad_v))):
        weights[side].start()
        for step in range(steps):
            part = pl.ds(step * CHUNK, CHUNK)
            copies.append(
                pltpu.make_async_copy(src.at[part], dst.at[part], x_sem.at[side * steps + step])
            )
            copies[-1].start()
    for side, (held, weight, out) in enumerate(((act_v, in_v, pa), (grad_v, out_v, pg))):
        weights[side].wait()
        for step in range(steps):
            part = pl.ds(step * CHUNK, CHUNK)
            copies[side * steps + step].wait()
            out[part, :] = lax.dot_general(
                held[part, :], weight[...], NT, preferred_element_type=jnp.float32
            ).astype(out.dtype)


def project(act, grad, w_in, w_out):
    rows, width = act.shape
    rank = w_in.shape[0]
    kind = act.dtype
    return pl.pallas_call(
        project_kernel,
        out_shape=[jax.ShapeDtypeStruct((rows, rank), kind)] * 2,
        in_specs=[HBM] * 4,
        out_specs=[VMEM] * 2,
        scratch_shapes=[
            pltpu.VMEM((rows, width), kind),
            pltpu.VMEM((rows, width), kind),
            pltpu.VMEM((rank, width), kind),
            pltpu.VMEM((rank, width), kind),
            pltpu.SemaphoreType.DMA((2,)),
            pltpu.SemaphoreType.DMA((2 * rows // CHUNK,)),
        ],
        compiler_params=pltpu.CompilerParams(vmem_limit_bytes=58 * 2**20),
        cost_estimate=pl.CostEstimate(
            flops=4 * rows * width * rank, bytes_accessed=4 * (rows + rank) * width, transcendentals=0
        ),
        name="project",
    )(act, grad, w_in, w_out)


def precond_kernel(block, got, own, other, out):
    total = jnp.dot(got[:, :block], own[...], preferred_element_type=jnp.float32)
    total += jnp.dot(got[:, block : 2 * block], other[...], preferred_element_type=jnp.float32)
    out[...] = total.astype(out.dtype)


def precondition(got, own, other):
    rows = got.shape[0]
    block, width = own.shape
    return pl.pallas_call(
        functools.partial(precond_kernel, block),
        out_shape=jax.ShapeDtypeStruct((rows, width), got.dtype),
        in_specs=[VMEM] * 3,
        out_specs=VMEM,
        compiler_params=pltpu.CompilerParams(vmem_limit_bytes=16 * 2**20),
        cost_estimate=pl.CostEstimate(
            flops=4 * rows * block * width, bytes_accessed=4 * block * width, transcendentals=0
        ),
        name="precondition",
    )(got, own, other)


def terms_kernel(chips, cols, fold, scale, precond, right, out):
    terms = lax.dot_general(precond[...], right[...], NT, preferred_element_type=jnp.float32) * scale
    tall, wide = terms.shape[0] // chips, terms.shape[1] // cols
    step = tall // fold
    for chip in range(chips):
        for col in range(cols):
            lanes = terms[chip * tall : (chip + 1) * tall, col * wide : (col + 1) * wide]
            out[chip * cols + col] = jnp.concatenate(
                [lanes[i * step : (i + 1) * step] for i in range(fold)], axis=1
            )


def kernel_terms(chips, cols, fold, scale, precond, right):
    rows, width = precond.shape
    other = right.shape[0]
    tall, wide = rows // chips, other // cols
    return pl.pallas_call(
        functools.partial(terms_kernel, chips, cols, fold, scale),
        out_shape=jax.ShapeDtypeStruct((chips * cols, tall // fold, fold * wide), jnp.float32),
        in_specs=[VMEM] * 2,
        out_specs=VMEM,
        compiler_params=pltpu.CompilerParams(vmem_limit_bytes=32 * 2**20),
        cost_estimate=pl.CostEstimate(
            flops=2 * rows * other * width, bytes_accessed=4 * rows * other, transcendentals=0
        ),
        name="kernel_terms",
    )(precond, right)


def per_device(chips, cols, activations, out_grads, proj_in, proj_out, inv_gram):
    seqs, length, width = activations.shape
    rank = proj_in.shape[1]
    feat = rank * rank
    row_block, col_block = inv_gram.shape
    plane = chips * cols
    half = seqs * plane
    tall = half // chips
    core = lax.axis_index("core")

    inv_other = other_core(inv_gram)

    proj_act, proj_grad = project(
        activations.reshape(seqs * length, width),
        out_grads.reshape(seqs * length, width),
        proj_in.T,
        proj_out.T,
    )
    proj_act = proj_act.reshape(seqs, length, rank)
    proj_grad = proj_grad.reshape(seqs, length, rank)
    summed = jnp.einsum(
        "sto,sti->soi", proj_grad, proj_act, preferred_element_type=jnp.float32
    ).reshape(seqs, feat)
    own_rows = (summed * (1.0 / math.sqrt(length))).astype(jnp.bfloat16)

    pieces = []
    for chip in range(chips):
        low = own_rows[:, 2 * chip * row_block : (2 * chip + 1) * row_block]
        high = own_rows[:, (2 * chip + 1) * row_block : (2 * chip + 2) * row_block]
        own, other = jnp.where(core == 0, low, high), jnp.where(core == 0, high, low)
        for col in range(cols):
            pieces.append(
                jnp.concatenate([own, other, own_rows[:, col * col_block : (col + 1) * col_block]], axis=1)
            )
    got = lax.all_to_all(jnp.stack(pieces), PLANE, 0, 0, tiled=True)
    got = got.reshape(half, 2 * row_block + col_block)

    mine = got[:, 2 * row_block :]
    theirs = other_core(mine)
    theirs, precond = lax.optimization_barrier((theirs, precondition(got, inv_gram, inv_other)))
    mine = mine.reshape(chips, 1, tall, col_block)
    theirs = theirs.reshape(chips, 1, tall, col_block)
    right = jnp.where(
        core == 0,
        jnp.concatenate([mine, theirs], axis=1),
        jnp.concatenate([theirs, mine], axis=1),
    ).reshape(2 * half, col_block)

    wide = 2 * half // cols
    fold = max(1, 128 // wide)
    terms = kernel_terms(chips, cols, fold, 8.0 / feat, precond, right)
    total = jnp.sum(lax.all_to_all(terms, PLANE, 0, 0, tiled=True), axis=0)
    return jnp.concatenate([total[:, i * wide : (i + 1) * wide] for i in range(fold)])


def solution(mesh):
    grp, gr, gc = (mesh.shape[name] for name in ("grp", "gr", "gc"))
    split = Mesh(mesh.devices.reshape(grp, gr // 2, 2, gc), ("grp", "chip", "core", "gc"))
    rows = ("grp", "chip", "core", "gc")
    in_specs = (P(rows, None, None), P(rows, None, None), P(), P(), P(("chip", "core"), "gc"))
    out_specs = P(("grp", "chip", "core"), "gc")

    def fn(*args):
        return per_device(gr // 2, gc, *args)

    return jax.shard_map(fn, mesh=split, in_specs=in_specs, out_specs=out_specs, check_vma=False)
```

```python
import functools
import math

import jax
import jax.numpy as jnp
from jax import lax
from jax.experimental import pallas as pl
from jax.experimental.pallas import tpu as pltpu
from jax.sharding import Mesh, PartitionSpec as P

PLANE = ("chip", "gc")
CHUNK = 1024
LIMIT = 57 * 2**20
VMEM = pl.BlockSpec(memory_space=pltpu.VMEM)
HBM = pl.BlockSpec(memory_space=pl.ANY)
NT = (((1,), (1,)), ((), ()))


def other_core(value):
    return lax.ppermute(value, "core", [(0, 1), (1, 0)])


def rows_kernel(length, act, grad, w_in, w_out, out, act_v, grad_v, in_v, out_v, w_sem, x_sem):
    seqs, rank = out.shape[:2]
    rows, width = act.shape
    steps = width // CHUNK
    sides = ((act, w_in, act_v, in_v), (grad, w_out, grad_v, out_v))
    copies = []
    for side, (x, w, x_v, w_v) in enumerate(sides):
        for step in range(steps):
            part = pl.ds(step * CHUNK, CHUNK)
            slot = side * steps + step
            pair = (
                pltpu.make_async_copy(w.at[:, part], w_v.at[:, part], w_sem.at[slot]),
                pltpu.make_async_copy(x.at[:, part], x_v.at[:, part], x_sem.at[slot]),
            )
            for copy in pair:
                copy.start()
            copies.append(pair)
    projected = []
    for side, (x, w, x_v, w_v) in enumerate(sides):
        total = jnp.zeros((rank, rows), jnp.float32)
        for step in range(steps):
            for copy in copies[side * steps + step]:
                copy.wait()
            part = pl.ds(step * CHUNK, CHUNK)
            total += lax.dot_general(
                w_v[:, part], x_v[:, part], NT, preferred_element_type=jnp.float32
            )
        projected.append(total.astype(out.dtype))
    proj_act, proj_grad = projected
    group = 128 // length
    place = lax.broadcasted_iota(jnp.int32, (rank, 128), 1) // length
    for first in range(0, seqs, group):
        tokens = slice(first * length, (first + group) * length)
        grads = proj_grad[:, tokens]
        left = jnp.concatenate(
            [jnp.where(place == i, grads, jnp.zeros_like(grads)) for i in range(group)]
        )
        summed = lax.dot_general(left, proj_act[:, tokens], NT, preferred_element_type=jnp.float32)
        summed = (summed * (1.0 / math.sqrt(length))).astype(out.dtype)
        out[first : first + group] = summed.reshape(group, rank, rank)


def gradient_rows(activations, out_grads, w_in, w_out):
    seqs, length, width = activations.shape
    rank = w_in.shape[0]
    rows = seqs * length
    kind = activations.dtype
    steps = 2 * width // CHUNK
    return pl.pallas_call(
        functools.partial(rows_kernel, length),
        out_shape=jax.ShapeDtypeStruct((seqs, rank, rank), kind),
        in_specs=[HBM] * 4,
        out_specs=VMEM,
        scratch_shapes=[
            pltpu.VMEM((rows, width), kind),
            pltpu.VMEM((rows, width), kind),
            pltpu.VMEM((rank, width), kind),
            pltpu.VMEM((rank, width), kind),
            pltpu.SemaphoreType.DMA((steps,)),
            pltpu.SemaphoreType.DMA((steps,)),
        ],
        compiler_params=pltpu.CompilerParams(vmem_limit_bytes=LIMIT),
        cost_estimate=pl.CostEstimate(
            flops=4 * rows * width * rank, bytes_accessed=4 * (rows + rank) * width, transcendentals=0
        ),
        name="gradient_rows",
    )(activations.reshape(rows, width), out_grads.reshape(rows, width), w_in, w_out)


def precond_kernel(block, got, own, other, out):
    total = jnp.dot(got[:, :block], own[...], preferred_element_type=jnp.float32)
    total += jnp.dot(got[:, block : 2 * block], other[...], preferred_element_type=jnp.float32)
    out[...] = total.astype(out.dtype)


def precondition(got, own, other):
    rows = got.shape[0]
    block, width = own.shape
    return pl.pallas_call(
        functools.partial(precond_kernel, block),
        out_shape=jax.ShapeDtypeStruct((rows, width), got.dtype),
        in_specs=[VMEM] * 3,
        out_specs=VMEM,
        compiler_params=pltpu.CompilerParams(vmem_limit_bytes=16 * 2**20),
        cost_estimate=pl.CostEstimate(
            flops=4 * rows * block * width, bytes_accessed=4 * block * width, transcendentals=0
        ),
        name="precondition",
    )(got, own, other)


def terms_kernel(chips, cols, fold, scale, precond, right, out):
    terms = lax.dot_general(precond[...], right[...], NT, preferred_element_type=jnp.float32) * scale
    tall, wide = terms.shape[0] // chips, terms.shape[1] // cols
    step = tall // fold
    for chip in range(chips):
        for col in range(cols):
            lanes = terms[chip * tall : (chip + 1) * tall, col * wide : (col + 1) * wide]
            out[chip * cols + col] = jnp.concatenate(
                [lanes[i * step : (i + 1) * step] for i in range(fold)], axis=1
            )


def kernel_terms(chips, cols, fold, scale, precond, right):
    rows, width = precond.shape
    other = right.shape[0]
    tall, wide = rows // chips, other // cols
    return pl.pallas_call(
        functools.partial(terms_kernel, chips, cols, fold, scale),
        out_shape=jax.ShapeDtypeStruct((chips * cols, tall // fold, fold * wide), jnp.float32),
        in_specs=[VMEM] * 2,
        out_specs=VMEM,
        compiler_params=pltpu.CompilerParams(vmem_limit_bytes=32 * 2**20),
        cost_estimate=pl.CostEstimate(
            flops=2 * rows * other * width, bytes_accessed=4 * rows * other, transcendentals=0
        ),
        name="kernel_terms",
    )(precond, right)


def per_device(chips, cols, activations, out_grads, proj_in, proj_out, inv_gram):
    seqs, length, width = activations.shape
    rank = proj_in.shape[1]
    feat = rank * rank
    row_block, col_block = inv_gram.shape
    plane = chips * cols
    half = seqs * plane
    tall = half // chips
    core = lax.axis_index("core")

    inv_other = other_core(inv_gram)

    own_rows = gradient_rows(activations, out_grads, proj_in.T, proj_out.T).reshape(seqs, feat)

    pieces = []
    for chip in range(chips):
        low = own_rows[:, 2 * chip * row_block : (2 * chip + 1) * row_block]
        high = own_rows[:, (2 * chip + 1) * row_block : (2 * chip + 2) * row_block]
        own, other = jnp.where(core == 0, low, high), jnp.where(core == 0, high, low)
        for col in range(cols):
            pieces.append(
                jnp.concatenate([own, other, own_rows[:, col * col_block : (col + 1) * col_block]], axis=1)
            )
    got = lax.all_to_all(jnp.stack(pieces), PLANE, 0, 0, tiled=True)
    got = got.reshape(half, 2 * row_block + col_block)

    mine = got[:, 2 * row_block :]
    theirs = other_core(mine)
    theirs, precond = lax.optimization_barrier((theirs, precondition(got, inv_gram, inv_other)))
    mine = mine.reshape(chips, 1, tall, col_block)
    theirs = theirs.reshape(chips, 1, tall, col_block)
    right = jnp.where(
        core == 0,
        jnp.concatenate([mine, theirs], axis=1),
        jnp.concatenate([theirs, mine], axis=1),
    ).reshape(2 * half, col_block)

    wide = 2 * half // cols
    fold = max(1, 128 // wide)
    terms = kernel_terms(chips, cols, fold, 8.0 / feat, precond, right)
    total = jnp.sum(lax.all_to_all(terms, PLANE, 0, 0, tiled=True), axis=0)
    return jnp.concatenate([total[:, i * wide : (i + 1) * wide] for i in range(fold)])


def solution(mesh):
    grp, gr, gc = (mesh.shape[name] for name in ("grp", "gr", "gc"))
    split = Mesh(mesh.devices.reshape(grp, gr // 2, 2, gc), ("grp", "chip", "core", "gc"))
    rows = ("grp", "chip", "core", "gc")
    in_specs = (P(rows, None, None), P(rows, None, None), P(), P(), P(("chip", "core"), "gc"))
    out_specs = P(("grp", "chip", "core"), "gc")

    def fn(*args):
        return per_device(gr // 2, gc, *args)

    return jax.shard_map(fn, mesh=split, in_specs=in_specs, out_specs=out_specs, check_vma=False)
```

```python
import functools
import math

import jax
import jax.numpy as jnp
from jax import lax
from jax.experimental import pallas as pl
from jax.experimental.pallas import tpu as pltpu
from jax.sharding import Mesh, PartitionSpec as P

PLANE = ("chip", "gc")
CHUNK = 1024
LIMIT = 107 * 2**19
VMEM = pl.BlockSpec(memory_space=pltpu.VMEM)
HBM = pl.BlockSpec(memory_space=pl.ANY)
NT = (((1,), (1,)), ((), ()))


def other_core(value):
    return lax.ppermute(value, "core", [(0, 1), (1, 0)])


def rows_kernel(length, act, grad, w_in, w_out, out, act_v, grad_v, in_v, out_v, w_sem, x_sem):
    seqs, rank = out.shape[:2]
    rows, width = act.shape
    steps = width // CHUNK
    sides = ((act, w_in, act_v, in_v), (grad, w_out, grad_v, out_v))
    copies = []
    for side, (x, w, x_v, w_v) in enumerate(sides):
        for step in range(steps):
            part = pl.ds(step * CHUNK, CHUNK)
            slot = side * steps + step
            pair = (
                pltpu.make_async_copy(w.at[:, part], w_v.at[:, part], w_sem.at[slot]),
                pltpu.make_async_copy(x.at[:, part], x_v.at[:, part], x_sem.at[slot]),
            )
            for copy in pair:
                copy.start()
            copies.append(pair)
    projected = []
    for side, (x, w, x_v, w_v) in enumerate(sides):
        total = jnp.zeros((rows, rank), jnp.float32)
        for step in range(steps):
            for copy in copies[side * steps + step]:
                copy.wait()
            part = pl.ds(step * CHUNK, CHUNK)
            total += lax.dot_general(
                x_v[:, part], w_v[:, part], NT, preferred_element_type=jnp.float32
            )
        projected.append(total)
    both = jnp.concatenate(projected, axis=1).T.astype(out.dtype)
    proj_act, proj_grad = both[:rank], both[rank:]
    group = 128 // length
    place = lax.broadcasted_iota(jnp.int32, (rank, 128), 1) // length
    for first in range(0, seqs, group):
        tokens = slice(first * length, (first + group) * length)
        grads = proj_grad[:, tokens]
        left = jnp.concatenate(
            [jnp.where(place == i, grads, jnp.zeros_like(grads)) for i in range(group)]
        )
        summed = lax.dot_general(left, proj_act[:, tokens], NT, preferred_element_type=jnp.float32)
        summed = (summed * (1.0 / math.sqrt(length))).astype(out.dtype)
        out[first : first + group] = summed.reshape(group, rank, rank)


def gradient_rows(activations, out_grads, w_in, w_out):
    seqs, length, width = activations.shape
    rank = w_in.shape[0]
    rows = seqs * length
    kind = activations.dtype
    steps = 2 * width // CHUNK
    return pl.pallas_call(
        functools.partial(rows_kernel, length),
        out_shape=jax.ShapeDtypeStruct((seqs, rank, rank), kind),
        in_specs=[HBM] * 4,
        out_specs=VMEM,
        scratch_shapes=[
            pltpu.VMEM((rows, width), kind),
            pltpu.VMEM((rows, width), kind),
            pltpu.VMEM((rank, width), kind),
            pltpu.VMEM((rank, width), kind),
            pltpu.SemaphoreType.DMA((steps,)),
            pltpu.SemaphoreType.DMA((steps,)),
        ],
        compiler_params=pltpu.CompilerParams(vmem_limit_bytes=LIMIT),
        cost_estimate=pl.CostEstimate(
            flops=4 * rows * width * rank, bytes_accessed=4 * (rows + rank) * width, transcendentals=0
        ),
        name="gradient_rows",
    )(activations.reshape(rows, width), out_grads.reshape(rows, width), w_in, w_out)


def precond_kernel(block, got, own, other, out):
    total = jnp.dot(got[:, :block], own[...], preferred_element_type=jnp.float32)
    total += jnp.dot(got[:, block : 2 * block], other[...], preferred_element_type=jnp.float32)
    out[...] = total.astype(out.dtype)


def precondition(got, own, other):
    rows = got.shape[0]
    block, width = own.shape
    return pl.pallas_call(
        functools.partial(precond_kernel, block),
        out_shape=jax.ShapeDtypeStruct((rows, width), got.dtype),
        in_specs=[VMEM] * 3,
        out_specs=VMEM,
        compiler_params=pltpu.CompilerParams(vmem_limit_bytes=16 * 2**20),
        cost_estimate=pl.CostEstimate(
            flops=4 * rows * block * width, bytes_accessed=4 * block * width, transcendentals=0
        ),
        name="precondition",
    )(got, own, other)


def terms_kernel(chips, cols, fold, scale, precond, right, out):
    terms = lax.dot_general(precond[...], right[...], NT, preferred_element_type=jnp.float32) * scale
    tall, wide = terms.shape[0] // chips, terms.shape[1] // cols
    step = tall // fold
    for chip in range(chips):
        for col in range(cols):
            lanes = terms[chip * tall : (chip + 1) * tall, col * wide : (col + 1) * wide]
            out[chip * cols + col] = jnp.concatenate(
                [lanes[i * step : (i + 1) * step] for i in range(fold)], axis=1
            )


def kernel_terms(chips, cols, fold, scale, precond, right):
    rows, width = precond.shape
    other = right.shape[0]
    tall, wide = rows // chips, other // cols
    return pl.pallas_call(
        functools.partial(terms_kernel, chips, cols, fold, scale),
        out_shape=jax.ShapeDtypeStruct((chips * cols, tall // fold, fold * wide), jnp.float32),
        in_specs=[VMEM] * 2,
        out_specs=VMEM,
        compiler_params=pltpu.CompilerParams(vmem_limit_bytes=32 * 2**20),
        cost_estimate=pl.CostEstimate(
            flops=2 * rows * other * width, bytes_accessed=4 * rows * other, transcendentals=0
        ),
        name="kernel_terms",
    )(precond, right)


def per_device(chips, cols, activations, out_grads, proj_in, proj_out, inv_gram):
    seqs, length, width = activations.shape
    rank = proj_in.shape[1]
    feat = rank * rank
    row_block, col_block = inv_gram.shape
    plane = chips * cols
    half = seqs * plane
    tall = half // chips
    core = lax.axis_index("core")

    inv_other = other_core(inv_gram)

    own_rows = gradient_rows(activations, out_grads, proj_in.T, proj_out.T).reshape(seqs, feat)

    pieces = []
    for chip in range(chips):
        low = own_rows[:, 2 * chip * row_block : (2 * chip + 1) * row_block]
        high = own_rows[:, (2 * chip + 1) * row_block : (2 * chip + 2) * row_block]
        own, other = jnp.where(core == 0, low, high), jnp.where(core == 0, high, low)
        for col in range(cols):
            pieces.append(
                jnp.concatenate([own, other, own_rows[:, col * col_block : (col + 1) * col_block]], axis=1)
            )
    got = lax.all_to_all(jnp.stack(pieces), PLANE, 0, 0, tiled=True)
    got = got.reshape(half, 2 * row_block + col_block)

    mine = got[:, 2 * row_block :]
    theirs = other_core(mine)
    theirs, precond = lax.optimization_barrier((theirs, precondition(got, inv_gram, inv_other)))
    mine = mine.reshape(chips, 1, tall, col_block)
    theirs = theirs.reshape(chips, 1, tall, col_block)
    right = jnp.where(
        core == 0,
        jnp.concatenate([mine, theirs], axis=1),
        jnp.concatenate([theirs, mine], axis=1),
    ).reshape(2 * half, col_block)

    wide = 2 * half // cols
    fold = max(1, 128 // wide)
    terms = kernel_terms(chips, cols, fold, 8.0 / feat, precond, right)
    total = jnp.sum(lax.all_to_all(terms, PLANE, 0, 0, tiled=True), axis=0)
    return jnp.concatenate([total[:, i * wide : (i + 1) * wide] for i in range(fold)])


def solution(mesh):
    grp, gr, gc = (mesh.shape[name] for name in ("grp", "gr", "gc"))
    split = Mesh(mesh.devices.reshape(grp, gr // 2, 2, gc), ("grp", "chip", "core", "gc"))
    rows = ("grp", "chip", "core", "gc")
    in_specs = (P(rows, None, None), P(rows, None, None), P(), P(), P(("chip", "core"), "gc"))
    out_specs = P(("grp", "chip", "core"), "gc")

    def fn(*args):
        return per_device(gr // 2, gc, *args)

    return jax.shard_map(fn, mesh=split, in_specs=in_specs, out_specs=out_specs, check_vma=False)
```

```python
import functools
import math

import jax
import jax.numpy as jnp
from jax import lax
from jax.experimental import pallas as pl
from jax.experimental.pallas import tpu as pltpu
from jax.sharding import Mesh, PartitionSpec as P

PLANE = ("chip", "gc")
CHUNK = 1024
LIMIT = 107 * 2**19
VMEM = pl.BlockSpec(memory_space=pltpu.VMEM)
HBM = pl.BlockSpec(memory_space=pl.ANY)
NT = (((1,), (1,)), ((), ()))


def other_core(value):
    return lax.ppermute(value, "core", [(0, 1), (1, 0)])


def left_parity(chip, col):
    home = col // 2
    return jnp.where(chip < home, col % 2, 1 - col % 2)


def rows_kernel(length, block, cols, act, grad, w_in, w_out, out, act_v, grad_v, in_v, out_v, w_sem, x_sem):
    seqs = out.shape[1]
    rank = w_in.shape[0]
    rows, width = act.shape
    steps = width // CHUNK
    sides = ((act, w_in, act_v, in_v), (grad, w_out, grad_v, out_v))
    copies = []
    for side, (x, w, x_v, w_v) in enumerate(sides):
        for step in range(steps):
            part = pl.ds(step * CHUNK, CHUNK)
            slot = side * steps + step
            pair = (
                pltpu.make_async_copy(w.at[:, part], w_v.at[:, part], w_sem.at[slot]),
                pltpu.make_async_copy(x.at[:, part], x_v.at[:, part], x_sem.at[slot]),
            )
            for copy in pair:
                copy.start()
            copies.append(pair)
    projected = []
    for side, (x, w, x_v, w_v) in enumerate(sides):
        total = jnp.zeros((rows, rank), jnp.float32)
        for step in range(steps):
            for copy in copies[side * steps + step]:
                copy.wait()
            part = pl.ds(step * CHUNK, CHUNK)
            total += lax.dot_general(
                x_v[:, part], w_v[:, part], NT, preferred_element_type=jnp.float32
            )
        projected.append(total)
    both = jnp.concatenate(projected, axis=1).T.astype(out.dtype)
    proj_act, proj_grad = both[:rank], both[rank:]
    many = rank // 2 * seqs
    row = lax.broadcasted_iota(jnp.int32, (many, rank), 0)
    column = lax.broadcasted_iota(jnp.int32, (many, rank), 1)
    token = lax.broadcasted_iota(jnp.int32, (many, rows), 1)
    sequence = lax.broadcasted_iota(jnp.int32, (many, rows), 0) % seqs
    left = []
    for odd in range(2):
        pick = (column == row // seqs * 2 + odd).astype(jnp.float32).astype(out.dtype)
        spread = jnp.dot(pick, proj_grad, preferred_element_type=jnp.float32)
        left.append(jnp.where(token // length == sequence, spread, 0.0).astype(out.dtype))
    nothing = jnp.zeros_like(proj_act)
    right = jnp.concatenate(
        [
            jnp.concatenate([proj_act, nothing], axis=1),
            jnp.concatenate([nothing, proj_act], axis=1),
        ]
    )
    summed = lax.dot_general(
        jnp.concatenate(left, axis=1), right, NT, preferred_element_type=jnp.float32
    )
    summed = summed * (1.0 / math.sqrt(length))
    lanes = 2 * rank
    tiles = block // lanes
    grad_rows = [
        summed[i * seqs : (i + 1) * seqs].astype(out.dtype) for i in range(many // seqs)
    ]
    for place in range(out.shape[0]):
        chip, col = place // cols, place % cols
        odd = col % 2 if chip < col // 2 else 1 - col % 2
        for slot, source in enumerate((2 * chip + odd, col)):
            for i in range(tiles):
                start = slot * block + i * lanes
                out[place, :, start : start + lanes] = grad_rows[source * tiles + i]


def gradient_pieces(plane, cols, block, activations, out_grads, w_in, w_out):
    seqs, length, width = activations.shape
    rank = w_in.shape[0]
    rows = seqs * length
    kind = activations.dtype
    steps = 2 * width // CHUNK
    return pl.pallas_call(
        functools.partial(rows_kernel, length, block, cols),
        out_shape=jax.ShapeDtypeStruct((plane, seqs, 2 * block), kind),
        in_specs=[HBM] * 4,
        out_specs=VMEM,
        scratch_shapes=[
            pltpu.VMEM((rows, width), kind),
            pltpu.VMEM((rows, width), kind),
            pltpu.VMEM((rank, width), kind),
            pltpu.VMEM((rank, width), kind),
            pltpu.SemaphoreType.DMA((steps,)),
            pltpu.SemaphoreType.DMA((steps,)),
        ],
        compiler_params=pltpu.CompilerParams(vmem_limit_bytes=LIMIT),
        cost_estimate=pl.CostEstimate(
            flops=4 * rows * width * rank, bytes_accessed=4 * (rows + rank) * width, transcendentals=0
        ),
        name="gradient_pieces",
    )(activations.reshape(rows, width), out_grads.reshape(rows, width), w_in, w_out)


def precond_kernel(block, weights, got, own, other, out):
    left = got[:, :block].astype(jnp.float32)
    right = got[:, block:].astype(jnp.float32)
    for_own = (left * weights[0] + right * weights[1]).astype(got.dtype)
    for_other = (left * weights[2] + right * weights[3]).astype(got.dtype)
    total = jnp.dot(for_own, own[...], preferred_element_type=jnp.float32)
    total += jnp.dot(for_other, other[...], preferred_element_type=jnp.float32)
    out[...] = total.astype(out.dtype)


def precondition(weights, got, own, other):
    rows = got.shape[0]
    block, width = own.shape
    return pl.pallas_call(
        functools.partial(precond_kernel, block),
        out_shape=jax.ShapeDtypeStruct((rows, width), got.dtype),
        in_specs=[pl.BlockSpec(memory_space=pltpu.SMEM)] + [VMEM] * 3,
        out_specs=VMEM,
        compiler_params=pltpu.CompilerParams(vmem_limit_bytes=16 * 2**20),
        cost_estimate=pl.CostEstimate(
            flops=4 * rows * block * width, bytes_accessed=4 * block * width, transcendentals=0
        ),
        name="precondition",
    )(weights, got, own, other)


def terms_kernel(n, fold, scale, core, precond, right, out):
    chips = n // 2
    size = right.shape[0] // n
    step = size // fold

    def packed(terms, row, col):
        lanes = terms[row * size : (row + 1) * size, col * size : (col + 1) * size]
        return jnp.concatenate([lanes[i * step : (i + 1) * step] for i in range(fold)], axis=1)

    def add(first, count):
        held = precond[pl.ds(first * size, count * size), :]
        once = lax.dot_general(held, right[...], NT, preferred_element_type=jnp.float32) * scale
        turned = lax.dot_general(right[...], held, NT, preferred_element_type=jnp.float32) * scale
        for chip in range(count):
            mine = 2 * (first + chip) + core[0]
            for place in range(n):
                out[mine * n + place] += packed(once, chip, place)
                out[place * n + mine] += packed(turned, place, chip)

    out[...] = jnp.zeros_like(out)
    if chips <= 2:
        add(0, chips)
    else:
        pl.loop(0, chips)(functools.partial(add, count=1))


def kernel_terms(n, fold, scale, core, precond, right):
    rows, width = precond.shape
    other = right.shape[0]
    size = other // n
    return pl.pallas_call(
        functools.partial(terms_kernel, n, fold, scale),
        out_shape=jax.ShapeDtypeStruct((n * n, size // fold, fold * size), jnp.float32),
        in_specs=[pl.BlockSpec(memory_space=pltpu.SMEM)] + [VMEM] * 2,
        out_specs=VMEM,
        compiler_params=pltpu.CompilerParams(
            vmem_limit_bytes=max(16 * 2**20, 12 * other * other)
        ),
        cost_estimate=pl.CostEstimate(
            flops=4 * rows * other * width, bytes_accessed=4 * other * other, transcendentals=0
        ),
        name="kernel_terms",
    )(core, precond, right)


def per_device(chips, cols, activations, out_grads, proj_in, proj_out, inv_gram):
    seqs, length, width = activations.shape
    rank = proj_in.shape[1]
    feat = rank * rank
    block = inv_gram.shape[0]
    plane = chips * cols
    half = seqs * plane
    tall = half // chips
    chip, core, col = (lax.axis_index(name) for name in ("chip", "core", "gc"))

    inv_other = other_core(inv_gram)

    pieces = gradient_pieces(plane, cols, block, activations, out_grads, proj_in.T, proj_out.T)
    got = lax.all_to_all(pieces, PLANE, 0, 0, tiled=True).reshape(half, 2 * block)

    mine = got[:, block:]
    theirs = other_core(mine)
    home = col // 2 == chip
    once = jnp.where(home & (col % 2 == 1), 0.0, 1.0)
    again = jnp.where(home, 0.5, 0.0)
    own_left = left_parity(chip, col) == core
    weights = jnp.stack(
        [
            jnp.where(own_left, once, 0.0),
            jnp.where(own_left, 0.0, again),
            jnp.where(own_left, 0.0, once),
            jnp.where(own_left, again, 0.0),
        ]
    ).astype(jnp.float32)
    theirs, precond = lax.optimization_barrier(
        (theirs, precondition(weights, got, inv_gram, inv_other))
    )
    mine = mine.reshape(chips, 1, tall, block)
    theirs = theirs.reshape(chips, 1, tall, block)
    right = jnp.where(
        core == 0,
        jnp.concatenate([mine, theirs], axis=1),
        jnp.concatenate([theirs, mine], axis=1),
    ).reshape(2 * half, block)

    fold = max(1, 128 // tall)
    terms = kernel_terms(cols, fold, 8.0 / feat, core.reshape(1).astype(jnp.int32), precond, right)
    total = jnp.sum(lax.all_to_all(terms, ("chip", "core", "gc"), 0, 0, tiled=True), axis=0)
    return jnp.concatenate([total[:, i * tall : (i + 1) * tall] for i in range(fold)])


def solution(mesh):
    grp, gr, gc = (mesh.shape[name] for name in ("grp", "gr", "gc"))
    split = Mesh(mesh.devices.reshape(grp, gr // 2, 2, gc), ("grp", "chip", "core", "gc"))
    rows = ("grp", "chip", "core", "gc")
    in_specs = (P(rows, None, None), P(rows, None, None), P(), P(), P(("chip", "core"), "gc"))
    out_specs = P(("grp", "chip", "core"), "gc")

    def fn(*args):
        return per_device(gr // 2, gc, *args)

    return jax.shard_map(fn, mesh=split, in_specs=in_specs, out_specs=out_specs, check_vma=False)
```

```python
import functools
import math

import jax
import jax.numpy as jnp
from jax import lax
from jax.experimental import pallas as pl
from jax.experimental.pallas import tpu as pltpu
from jax.sharding import Mesh, PartitionSpec as P

PLANE = ("chip", "gc")
CHUNK = 1024
LIMIT = 107 * 2**19
VMEM = pl.BlockSpec(memory_space=pltpu.VMEM)
HBM = pl.BlockSpec(memory_space=pl.ANY)
NT = (((1,), (1,)), ((), ()))


def other_core(value):
    return lax.ppermute(value, "core", [(0, 1), (1, 0)])


def left_parity(chip, col):
    home = col // 2
    return jnp.where(chip < home, col % 2, 1 - col % 2)


def rows_kernel(length, block, cols, act, grad, w_in, w_out, out, act_v, grad_v, in_v, out_v, w_sem, x_sem):
    seqs = out.shape[1]
    rank = w_in.shape[0]
    rows, width = act.shape
    steps = width // CHUNK
    sides = ((act, w_in, act_v, in_v), (grad, w_out, grad_v, out_v))
    copies = []
    for side, (x, w, x_v, w_v) in enumerate(sides):
        for step in range(steps):
            part = pl.ds(step * CHUNK, CHUNK)
            slot = side * steps + step
            pair = (
                pltpu.make_async_copy(w.at[:, part], w_v.at[:, part], w_sem.at[slot]),
                pltpu.make_async_copy(x.at[:, part], x_v.at[:, part], x_sem.at[slot]),
            )
            for copy in pair:
                copy.start()
            copies.append(pair)
    projected = []
    for side, (x, w, x_v, w_v) in enumerate(sides):
        total = jnp.zeros((rows, rank), jnp.float32)
        for step in range(steps):
            for copy in copies[side * steps + step]:
                copy.wait()
            part = pl.ds(step * CHUNK, CHUNK)
            total += lax.dot_general(
                x_v[:, part], w_v[:, part], NT, preferred_element_type=jnp.float32
            )
        projected.append(total)
    both = jnp.concatenate(projected, axis=1).T.astype(out.dtype)
    proj_act, proj_grad = both[:rank], both[rank:]
    many = rank // 2 * seqs
    row = lax.broadcasted_iota(jnp.int32, (many, rank), 0)
    column = lax.broadcasted_iota(jnp.int32, (many, rank), 1)
    token = lax.broadcasted_iota(jnp.int32, (many, rows), 1)
    sequence = lax.broadcasted_iota(jnp.int32, (many, rows), 0) % seqs
    left = []
    for odd in range(2):
        pick = (column == row // seqs * 2 + odd).astype(jnp.float32).astype(out.dtype)
        spread = jnp.dot(pick, proj_grad, preferred_element_type=jnp.float32)
        left.append(jnp.where(token // length == sequence, spread, 0.0).astype(out.dtype))
    nothing = jnp.zeros_like(proj_act)
    right = jnp.concatenate(
        [
            jnp.concatenate([proj_act, nothing], axis=1),
            jnp.concatenate([nothing, proj_act], axis=1),
        ]
    )
    summed = lax.dot_general(
        jnp.concatenate(left, axis=1), right, NT, preferred_element_type=jnp.float32
    )
    summed = summed * (1.0 / math.sqrt(length))
    lanes = 2 * rank
    tiles = block // lanes
    grad_rows = [
        summed[i * seqs : (i + 1) * seqs].astype(out.dtype) for i in range(many // seqs)
    ]
    for place in range(out.shape[0]):
        chip, col = place // cols, place % cols
        odd = col % 2 if chip < col // 2 else 1 - col % 2
        for slot, source in enumerate((2 * chip + odd, col)):
            for i in range(tiles):
                start = slot * block + i * lanes
                out[place, :, start : start + lanes] = grad_rows[source * tiles + i]


def gradient_pieces(plane, cols, block, activations, out_grads, w_in, w_out):
    seqs, length, width = activations.shape
    rank = w_in.shape[0]
    rows = seqs * length
    kind = activations.dtype
    steps = 2 * width // CHUNK
    return pl.pallas_call(
        functools.partial(rows_kernel, length, block, cols),
        out_shape=jax.ShapeDtypeStruct((plane, seqs, 2 * block), kind),
        in_specs=[HBM] * 4,
        out_specs=VMEM,
        scratch_shapes=[
            pltpu.VMEM((rows, width), kind),
            pltpu.VMEM((rows, width), kind),
            pltpu.VMEM((rank, width), kind),
            pltpu.VMEM((rank, width), kind),
            pltpu.SemaphoreType.DMA((steps,)),
            pltpu.SemaphoreType.DMA((steps,)),
        ],
        compiler_params=pltpu.CompilerParams(vmem_limit_bytes=LIMIT),
        cost_estimate=pl.CostEstimate(
            flops=4 * rows * width * rank, bytes_accessed=4 * (rows + rank) * width, transcendentals=0
        ),
        name="gradient_pieces",
    )(activations.reshape(rows, width), out_grads.reshape(rows, width), w_in, w_out)


def precond_kernel(block, weights, got, own, other, out):
    left = got[:, :block].astype(jnp.float32)
    right = got[:, block:].astype(jnp.float32)
    for_own = (left * weights[0] + right * weights[1]).astype(got.dtype)
    for_other = (left * weights[2] + right * weights[3]).astype(got.dtype)
    total = jnp.dot(for_own, own[...], preferred_element_type=jnp.float32)
    total += jnp.dot(for_other, other[...], preferred_element_type=jnp.float32)
    out[...] = total.astype(out.dtype)


def precondition(weights, got, own, other):
    rows = got.shape[0]
    block, width = own.shape
    return pl.pallas_call(
        functools.partial(precond_kernel, block),
        out_shape=jax.ShapeDtypeStruct((rows, width), got.dtype),
        in_specs=[pl.BlockSpec(memory_space=pltpu.SMEM)] + [VMEM] * 3,
        out_specs=VMEM,
        compiler_params=pltpu.CompilerParams(vmem_limit_bytes=16 * 2**20),
        cost_estimate=pl.CostEstimate(
            flops=4 * rows * block * width, bytes_accessed=4 * block * width, transcendentals=0
        ),
        name="precondition",
    )(weights, got, own, other)


def terms_kernel(n, fold, scale, core, precond, right, out):
    chips = n // 2
    size = right.shape[0] // n
    step = size // fold

    def packed(terms, row, col):
        lanes = terms[row * size : (row + 1) * size, col * size : (col + 1) * size]
        return jnp.concatenate([lanes[i * step : (i + 1) * step] for i in range(fold)], axis=1)

    def add(first, count):
        held = precond[pl.ds(first * size, count * size), :]
        once = lax.dot_general(held, right[...], NT, preferred_element_type=jnp.float32) * scale
        turned = lax.dot_general(right[...], held, NT, preferred_element_type=jnp.float32) * scale
        for chip in range(count):
            mine = 2 * (first + chip) + core[0]
            for place in range(n):
                out[mine * n + place] += packed(once, chip, place)
                out[place * n + mine] += packed(turned, place, chip)

    out[...] = jnp.zeros_like(out)
    if chips <= 2:
        add(0, chips)
    else:
        pl.loop(0, chips)(functools.partial(add, count=1))


def kernel_terms(n, fold, scale, core, precond, right):
    rows, width = precond.shape
    other = right.shape[0]
    size = other // n
    return pl.pallas_call(
        functools.partial(terms_kernel, n, fold, scale),
        out_shape=jax.ShapeDtypeStruct((n * n, size // fold, fold * size), jnp.float32),
        in_specs=[pl.BlockSpec(memory_space=pltpu.SMEM)] + [VMEM] * 2,
        out_specs=VMEM,
        compiler_params=pltpu.CompilerParams(
            vmem_limit_bytes=max(16 * 2**20, 12 * other * other)
        ),
        cost_estimate=pl.CostEstimate(
            flops=4 * rows * other * width, bytes_accessed=4 * other * other, transcendentals=0
        ),
        name="kernel_terms",
    )(core, precond, right)


def per_device(chips, cols, activations, out_grads, proj_in, proj_out, inv_gram):
    seqs, length, width = activations.shape
    rank = proj_in.shape[1]
    feat = rank * rank
    block = inv_gram.shape[0]
    plane = chips * cols
    half = seqs * plane
    tall = half // chips
    chip, core, col = (lax.axis_index(name) for name in ("chip", "core", "gc"))

    pieces = gradient_pieces(plane, cols, block, activations, out_grads, proj_in.T, proj_out.T)
    pieces, inv_gram = lax.optimization_barrier((pieces, inv_gram))
    inv_other = other_core(inv_gram)
    got = lax.all_to_all(pieces, PLANE, 0, 0, tiled=True).reshape(half, 2 * block)

    mine = got[:, block:]
    theirs = other_core(mine)
    home = col // 2 == chip
    once = jnp.where(home & (col % 2 == 1), 0.0, 1.0)
    again = jnp.where(home, 0.5, 0.0)
    own_left = left_parity(chip, col) == core
    weights = jnp.stack(
        [
            jnp.where(own_left, once, 0.0),
            jnp.where(own_left, 0.0, again),
            jnp.where(own_left, 0.0, once),
            jnp.where(own_left, again, 0.0),
        ]
    ).astype(jnp.float32)
    theirs, precond = lax.optimization_barrier(
        (theirs, precondition(weights, got, inv_gram, inv_other))
    )
    mine = mine.reshape(chips, 1, tall, block)
    theirs = theirs.reshape(chips, 1, tall, block)
    right = jnp.where(
        core == 0,
        jnp.concatenate([mine, theirs], axis=1),
        jnp.concatenate([theirs, mine], axis=1),
    ).reshape(2 * half, block)

    fold = max(1, 128 // tall)
    terms = kernel_terms(cols, fold, 8.0 / feat, core.reshape(1).astype(jnp.int32), precond, right)
    total = jnp.sum(lax.all_to_all(terms, ("chip", "core", "gc"), 0, 0, tiled=True), axis=0)
    return jnp.concatenate([total[:, i * tall : (i + 1) * tall] for i in range(fold)])


def solution(mesh):
    grp, gr, gc = (mesh.shape[name] for name in ("grp", "gr", "gc"))
    split = Mesh(mesh.devices.reshape(grp, gr // 2, 2, gc), ("grp", "chip", "core", "gc"))
    rows = ("grp", "chip", "core", "gc")
    in_specs = (P(rows, None, None), P(rows, None, None), P(), P(), P(("chip", "core"), "gc"))
    out_specs = P(("grp", "chip", "core"), "gc")

    def fn(*args):
        return per_device(gr // 2, gc, *args)

    return jax.shard_map(fn, mesh=split, in_specs=in_specs, out_specs=out_specs, check_vma=False)
```

```python
import functools
import math

import jax
import jax.numpy as jnp
from jax import lax
from jax.experimental import pallas as pl
from jax.experimental.pallas import tpu as pltpu
from jax.sharding import Mesh, PartitionSpec as P

PLANE = ("chip", "gc")
CHUNK = 1024
PARTS = 2
LIMIT = 107 * 2**19
VMEM = pl.BlockSpec(memory_space=pltpu.VMEM)
HBM = pl.BlockSpec(memory_space=pl.ANY)
NT = (((1,), (1,)), ((), ()))


def other_core(value):
    return lax.ppermute(value, "core", [(0, 1), (1, 0)])


def left_parity(chip, col):
    home = col // 2
    return jnp.where(chip < home, col % 2, 1 - col % 2)


def rows_kernel(length, block, cols, act, grad, w_in, w_out, out, act_v, grad_v, in_v, out_v, w_sem, x_sem):
    seqs = out.shape[1]
    rank = w_in.shape[0]
    rows, width = act.shape
    steps = width // CHUNK
    sides = ((grad, w_out, grad_v, out_v), (act, w_in, act_v, in_v))
    copies = []
    for side, (x, w, x_v, w_v) in enumerate(sides):
        for step in range(steps):
            part = pl.ds(step * CHUNK, CHUNK)
            slot = side * steps + step
            pair = (
                pltpu.make_async_copy(w.at[:, part], w_v.at[:, part], w_sem.at[slot]),
                pltpu.make_async_copy(x.at[:, part], x_v.at[:, part], x_sem.at[slot]),
            )
            for copy in pair:
                copy.start()
            copies.append(pair)

    def projected(side):
        _, _, x_v, w_v = sides[side]
        total = jnp.zeros((rows, rank), jnp.float32)
        for step in range(steps):
            for copy in copies[side * steps + step]:
                copy.wait()
            part = pl.ds(step * CHUNK, CHUNK)
            total += lax.dot_general(
                x_v[:, part], w_v[:, part], NT, preferred_element_type=jnp.float32
            )
        return total.astype(out.dtype)

    proj_grad = projected(0)
    many = rank // 2 * seqs
    row = lax.broadcasted_iota(jnp.int32, (many, rank), 0)
    column = lax.broadcasted_iota(jnp.int32, (many, rank), 1)
    token = lax.broadcasted_iota(jnp.int32, (many, rows), 1)
    sequence = lax.broadcasted_iota(jnp.int32, (many, rows), 0) % seqs
    left = []
    for odd in range(2):
        pick = (column == row // seqs * 2 + odd).astype(jnp.float32).astype(out.dtype)
        spread = lax.dot_general(pick, proj_grad, NT, preferred_element_type=jnp.float32)
        left.append(jnp.where(token // length == sequence, spread, 0.0).astype(out.dtype))
    left = jnp.concatenate(left, axis=1)
    proj_act = projected(1)
    nothing = jnp.zeros_like(proj_act)
    right = jnp.concatenate(
        [
            jnp.concatenate([proj_act, nothing], axis=1),
            jnp.concatenate([nothing, proj_act], axis=1),
        ]
    )
    summed = jnp.dot(left, right, preferred_element_type=jnp.float32)
    summed = summed * (1.0 / math.sqrt(length))
    lanes = 2 * rank
    tiles = block // lanes
    grad_rows = [
        summed[i * seqs : (i + 1) * seqs].astype(out.dtype) for i in range(many // seqs)
    ]
    for place in range(out.shape[0]):
        chip, col = place // cols, place % cols
        odd = col % 2 if chip < col // 2 else 1 - col % 2
        for slot, source in enumerate((2 * chip + odd, col)):
            for i in range(tiles):
                start = slot * block + i * lanes
                out[place, :, start : start + lanes] = grad_rows[source * tiles + i]


def gradient_pieces(plane, cols, block, activations, out_grads, w_in, w_out):
    seqs, length, width = activations.shape
    rank = w_in.shape[0]
    rows = seqs * length
    kind = activations.dtype
    steps = 2 * width // CHUNK
    return pl.pallas_call(
        functools.partial(rows_kernel, length, block, cols),
        out_shape=jax.ShapeDtypeStruct((plane, seqs, 2 * block), kind),
        in_specs=[HBM] * 4,
        out_specs=VMEM,
        scratch_shapes=[
            pltpu.VMEM((rows, width), kind),
            pltpu.VMEM((rows, width), kind),
            pltpu.VMEM((rank, width), kind),
            pltpu.VMEM((rank, width), kind),
            pltpu.SemaphoreType.DMA((steps,)),
            pltpu.SemaphoreType.DMA((steps,)),
        ],
        compiler_params=pltpu.CompilerParams(vmem_limit_bytes=LIMIT),
        cost_estimate=pl.CostEstimate(
            flops=4 * rows * width * rank, bytes_accessed=4 * (rows + rank) * width, transcendentals=0
        ),
        name="gradient_pieces",
    )(activations.reshape(rows, width), out_grads.reshape(rows, width), w_in, w_out)


def precond_kernel(block, weights, got, own, other, out, other_v, sem):
    step = block // PARTS
    copies = []
    for i in range(PARTS):
        part = pl.ds(i * step, step)
        copies.append(pltpu.make_async_copy(other.at[part], other_v.at[part], sem.at[i]))
        copies[-1].start()
    left = got[:, :block].astype(jnp.float32)
    right = got[:, block:].astype(jnp.float32)
    for_own = (left * weights[0] + right * weights[1]).astype(got.dtype)
    for_other = (left * weights[2] + right * weights[3]).astype(got.dtype)
    total = jnp.dot(for_own, own[...], preferred_element_type=jnp.float32)
    for i in range(PARTS):
        copies[i].wait()
        part = slice(i * step, (i + 1) * step)
        total += jnp.dot(for_other[:, part], other_v[part, :], preferred_element_type=jnp.float32)
    out[...] = total.astype(out.dtype)


def precondition(weights, got, own, other):
    rows = got.shape[0]
    block, width = own.shape
    return pl.pallas_call(
        functools.partial(precond_kernel, block),
        out_shape=jax.ShapeDtypeStruct((rows, width), got.dtype),
        in_specs=[pl.BlockSpec(memory_space=pltpu.SMEM), VMEM, VMEM, HBM],
        out_specs=VMEM,
        scratch_shapes=[pltpu.VMEM(other.shape, other.dtype), pltpu.SemaphoreType.DMA((PARTS,))],
        compiler_params=pltpu.CompilerParams(vmem_limit_bytes=16 * 2**20),
        cost_estimate=pl.CostEstimate(
            flops=4 * rows * block * width, bytes_accessed=4 * block * width, transcendentals=0
        ),
        name="precondition",
    )(weights, got, own, other)


def terms_kernel(n, fold, scale, core, precond, right, out):
    chips = n // 2
    size = right.shape[0] // n
    step = size // fold

    def packed(terms, row, col):
        lanes = terms[row * size : (row + 1) * size, col * size : (col + 1) * size]
        return jnp.concatenate([lanes[i * step : (i + 1) * step] for i in range(fold)], axis=1)

    def add(first, count):
        held = precond[pl.ds(first * size, count * size), :]
        once = lax.dot_general(held, right[...], NT, preferred_element_type=jnp.float32) * scale
        turned = lax.dot_general(right[...], held, NT, preferred_element_type=jnp.float32) * scale
        for chip in range(count):
            mine = 2 * (first + chip) + core[0]
            for place in range(n):
                out[mine * n + place] += packed(once, chip, place)
                out[place * n + mine] += packed(turned, place, chip)

    out[...] = jnp.zeros_like(out)
    if chips <= 2:
        add(0, chips)
    else:
        pl.loop(0, chips)(functools.partial(add, count=1))


def kernel_terms(n, fold, scale, core, precond, right):
    rows, width = precond.shape
    other = right.shape[0]
    size = other // n
    return pl.pallas_call(
        functools.partial(terms_kernel, n, fold, scale),
        out_shape=jax.ShapeDtypeStruct((n * n, size // fold, fold * size), jnp.float32),
        in_specs=[pl.BlockSpec(memory_space=pltpu.SMEM)] + [VMEM] * 2,
        out_specs=VMEM,
        compiler_params=pltpu.CompilerParams(
            vmem_limit_bytes=max(16 * 2**20, 12 * other * other)
        ),
        cost_estimate=pl.CostEstimate(
            flops=4 * rows * other * width, bytes_accessed=4 * other * other, transcendentals=0
        ),
        name="kernel_terms",
    )(core, precond, right)


def per_device(chips, cols, activations, out_grads, proj_in, proj_out, inv_gram):
    seqs, length, width = activations.shape
    rank = proj_in.shape[1]
    feat = rank * rank
    block = inv_gram.shape[0]
    plane = chips * cols
    half = seqs * plane
    tall = half // chips
    chip, core, col = (lax.axis_index(name) for name in ("chip", "core", "gc"))

    inv_other = other_core(inv_gram)

    pieces = gradient_pieces(plane, cols, block, activations, out_grads, proj_in.T, proj_out.T)
    got = lax.all_to_all(pieces, PLANE, 0, 0, tiled=True).reshape(half, 2 * block)

    mine = got[:, block:]
    theirs = other_core(mine)
    home = col // 2 == chip
    once = jnp.where(home & (col % 2 == 1), 0.0, 1.0)
    again = jnp.where(home, 0.5, 0.0)
    own_left = left_parity(chip, col) == core
    weights = jnp.stack(
        [
            jnp.where(own_left, once, 0.0),
            jnp.where(own_left, 0.0, again),
            jnp.where(own_left, 0.0, once),
            jnp.where(own_left, again, 0.0),
        ]
    ).astype(jnp.float32)
    theirs, precond = lax.optimization_barrier(
        (theirs, precondition(weights, got, inv_gram, inv_other))
    )
    mine = mine.reshape(chips, 1, tall, block)
    theirs = theirs.reshape(chips, 1, tall, block)
    right = jnp.where(
        core == 0,
        jnp.concatenate([mine, theirs], axis=1),
        jnp.concatenate([theirs, mine], axis=1),
    ).reshape(2 * half, block)

    fold = max(1, 128 // tall)
    terms = kernel_terms(cols, fold, 8.0 / feat, core.reshape(1).astype(jnp.int32), precond, right)
    total = jnp.sum(lax.all_to_all(terms, ("chip", "core", "gc"), 0, 0, tiled=True), axis=0)
    return jnp.concatenate([total[:, i * tall : (i + 1) * tall] for i in range(fold)])


def solution(mesh):
    grp, gr, gc = (mesh.shape[name] for name in ("grp", "gr", "gc"))
    split = Mesh(mesh.devices.reshape(grp, gr // 2, 2, gc), ("grp", "chip", "core", "gc"))
    rows = ("grp", "chip", "core", "gc")
    in_specs = (P(rows, None, None), P(rows, None, None), P(), P(), P(("chip", "core"), "gc"))
    out_specs = P(("grp", "chip", "core"), "gc")

    def fn(*args):
        return per_device(gr // 2, gc, *args)

    return jax.shard_map(fn, mesh=split, in_specs=in_specs, out_specs=out_specs, check_vma=False)
```

```python
import functools
import math

import jax
import jax.numpy as jnp
from jax import lax
from jax.experimental import pallas as pl
from jax.experimental.pallas import tpu as pltpu
from jax.sharding import Mesh, PartitionSpec as P

PLANE = ("chip", "gc")
CHUNK = 1024
LIMIT = 107 * 2**19
VMEM = pl.BlockSpec(memory_space=pltpu.VMEM)
HBM = pl.BlockSpec(memory_space=pl.ANY)
NT = (((1,), (1,)), ((), ()))


def other_core(value):
    return lax.ppermute(value, "core", [(0, 1), (1, 0)])


def left_parity(chip, col):
    home = col // 2
    return jnp.where(chip < home, col % 2, 1 - col % 2)


def rows_kernel(length, block, cols, act, grad, w_in, w_out, out, x_v, w_v, w_sem, x_sem):
    seqs = out.shape[1]
    rank = w_in.shape[0]
    rows, width = act.shape
    weights = [
        pltpu.make_async_copy(w, w_v.at[pl.ds(side * rank, rank)], w_sem.at[side])
        for side, w in enumerate((w_in, w_out))
    ]
    copies = []
    for step in range(width // CHUNK):
        part = pl.ds(step * CHUNK, CHUNK)
        copies.append(
            [
                pltpu.make_async_copy(
                    x.at[:, part], x_v.at[pl.ds(side * rows, rows), part], x_sem.at[step, side]
                )
                for side, x in enumerate((act, grad))
            ]
        )
    for copy in weights + sum(copies, []):
        copy.start()
    total = jnp.zeros((2 * rank, 2 * rows), jnp.float32)
    for copy in weights:
        copy.wait()
    for step, pair in enumerate(copies):
        for copy in pair:
            copy.wait()
        part = pl.ds(step * CHUNK, CHUNK)
        total += lax.dot_general(
            w_v[:, part], x_v[:, part], NT, preferred_element_type=jnp.float32
        )
    proj_act = total[:rank, :rows].astype(out.dtype)
    proj_grad = total[rank:, rows:].astype(out.dtype)
    many = rank // 2 * seqs
    row = lax.broadcasted_iota(jnp.int32, (many, rank), 0)
    column = lax.broadcasted_iota(jnp.int32, (many, rank), 1)
    token = lax.broadcasted_iota(jnp.int32, (many, rows), 1)
    sequence = lax.broadcasted_iota(jnp.int32, (many, rows), 0) % seqs
    left = []
    for odd in range(2):
        pick = (column == row // seqs * 2 + odd).astype(jnp.float32).astype(out.dtype)
        spread = jnp.dot(pick, proj_grad, preferred_element_type=jnp.float32)
        left.append(jnp.where(token // length == sequence, spread, 0.0).astype(out.dtype))
    nothing = jnp.zeros_like(proj_act)
    right = jnp.concatenate(
        [
            jnp.concatenate([proj_act, nothing], axis=1),
            jnp.concatenate([nothing, proj_act], axis=1),
        ]
    )
    summed = lax.dot_general(
        jnp.concatenate(left, axis=1), right, NT, preferred_element_type=jnp.float32
    )
    summed = summed * (1.0 / math.sqrt(length))
    lanes = 2 * rank
    tiles = block // lanes
    grad_rows = [
        summed[i * seqs : (i + 1) * seqs].astype(out.dtype) for i in range(many // seqs)
    ]
    for place in range(out.shape[0]):
        chip, col = place // cols, place % cols
        odd = col % 2 if chip < col // 2 else 1 - col % 2
        for slot, source in enumerate((2 * chip + odd, col)):
            for i in range(tiles):
                start = slot * block + i * lanes
                out[place, :, start : start + lanes] = grad_rows[source * tiles + i]


def gradient_pieces(plane, cols, block, activations, out_grads, w_in, w_out):
    seqs, length, width = activations.shape
    rank = w_in.shape[0]
    rows = seqs * length
    kind = activations.dtype
    return pl.pallas_call(
        functools.partial(rows_kernel, length, block, cols),
        out_shape=jax.ShapeDtypeStruct((plane, seqs, 2 * block), kind),
        in_specs=[HBM] * 4,
        out_specs=VMEM,
        scratch_shapes=[
            pltpu.VMEM((2 * rows, width), kind),
            pltpu.VMEM((2 * rank, width), kind),
            pltpu.SemaphoreType.DMA((2,)),
            pltpu.SemaphoreType.DMA((width // CHUNK, 2)),
        ],
        compiler_params=pltpu.CompilerParams(vmem_limit_bytes=LIMIT),
        cost_estimate=pl.CostEstimate(
            flops=8 * rows * width * rank, bytes_accessed=4 * (rows + rank) * width, transcendentals=0
        ),
        name="gradient_pieces",
    )(activations.reshape(rows, width), out_grads.reshape(rows, width), w_in, w_out)


def precond_kernel(block, weights, got, own, other, out):
    left = got[:, :block].astype(jnp.float32)
    right = got[:, block:].astype(jnp.float32)
    for_own = (left * weights[0] + right * weights[1]).astype(got.dtype)
    for_other = (left * weights[2] + right * weights[3]).astype(got.dtype)
    total = jnp.dot(for_own, own[...], preferred_element_type=jnp.float32)
    total += jnp.dot(for_other, other[...], preferred_element_type=jnp.float32)
    out[...] = total.astype(out.dtype)


def precondition(weights, got, own, other):
    rows = got.shape[0]
    block, width = own.shape
    return pl.pallas_call(
        functools.partial(precond_kernel, block),
        out_shape=jax.ShapeDtypeStruct((rows, width), got.dtype),
        in_specs=[pl.BlockSpec(memory_space=pltpu.SMEM)] + [VMEM] * 3,
        out_specs=VMEM,
        compiler_params=pltpu.CompilerParams(vmem_limit_bytes=16 * 2**20),
        cost_estimate=pl.CostEstimate(
            flops=4 * rows * block * width, bytes_accessed=4 * block * width, transcendentals=0
        ),
        name="precondition",
    )(weights, got, own, other)


def terms_kernel(n, fold, scale, core, precond, right, out):
    chips = n // 2
    size = right.shape[0] // n
    step = size // fold

    def packed(terms, row, col):
        lanes = terms[row * size : (row + 1) * size, col * size : (col + 1) * size]
        return jnp.concatenate([lanes[i * step : (i + 1) * step] for i in range(fold)], axis=1)

    def add(first, count):
        held = precond[pl.ds(first * size, count * size), :]
        once = lax.dot_general(held, right[...], NT, preferred_element_type=jnp.float32) * scale
        turned = lax.dot_general(right[...], held, NT, preferred_element_type=jnp.float32) * scale
        for chip in range(count):
            mine = 2 * (first + chip) + core[0]
            for place in range(n):
                out[mine * n + place] += packed(once, chip, place)
                out[place * n + mine] += packed(turned, place, chip)

    out[...] = jnp.zeros_like(out)
    if chips <= 2:
        add(0, chips)
    else:
        pl.loop(0, chips)(functools.partial(add, count=1))


def kernel_terms(n, fold, scale, core, precond, right):
    rows, width = precond.shape
    other = right.shape[0]
    size = other // n
    return pl.pallas_call(
        functools.partial(terms_kernel, n, fold, scale),
        out_shape=jax.ShapeDtypeStruct((n * n, size // fold, fold * size), jnp.float32),
        in_specs=[pl.BlockSpec(memory_space=pltpu.SMEM)] + [VMEM] * 2,
        out_specs=VMEM,
        compiler_params=pltpu.CompilerParams(
            vmem_limit_bytes=max(16 * 2**20, 12 * other * other)
        ),
        cost_estimate=pl.CostEstimate(
            flops=4 * rows * other * width, bytes_accessed=4 * other * other, transcendentals=0
        ),
        name="kernel_terms",
    )(core, precond, right)


def per_device(chips, cols, activations, out_grads, proj_in, proj_out, inv_gram):
    seqs, length, width = activations.shape
    rank = proj_in.shape[1]
    feat = rank * rank
    block = inv_gram.shape[0]
    plane = chips * cols
    half = seqs * plane
    tall = half // chips
    chip, core, col = (lax.axis_index(name) for name in ("chip", "core", "gc"))

    inv_other = other_core(inv_gram)

    pieces = gradient_pieces(plane, cols, block, activations, out_grads, proj_in.T, proj_out.T)
    got = lax.all_to_all(pieces, PLANE, 0, 0, tiled=True).reshape(half, 2 * block)

    mine = got[:, block:]
    theirs = other_core(mine)
    home = col // 2 == chip
    once = jnp.where(home & (col % 2 == 1), 0.0, 1.0)
    again = jnp.where(home, 0.5, 0.0)
    own_left = left_parity(chip, col) == core
    weights = jnp.stack(
        [
            jnp.where(own_left, once, 0.0),
            jnp.where(own_left, 0.0, again),
            jnp.where(own_left, 0.0, once),
            jnp.where(own_left, again, 0.0),
        ]
    ).astype(jnp.float32)
    theirs, precond = lax.optimization_barrier(
        (theirs, precondition(weights, got, inv_gram, inv_other))
    )
    mine = mine.reshape(chips, 1, tall, block)
    theirs = theirs.reshape(chips, 1, tall, block)
    right = jnp.where(
        core == 0,
        jnp.concatenate([mine, theirs], axis=1),
        jnp.concatenate([theirs, mine], axis=1),
    ).reshape(2 * half, block)

    fold = max(1, 128 // tall)
    terms = kernel_terms(cols, fold, 8.0 / feat, core.reshape(1).astype(jnp.int32), precond, right)
    total = jnp.sum(lax.all_to_all(terms, ("chip", "core", "gc"), 0, 0, tiled=True), axis=0)
    return jnp.concatenate([total[:, i * tall : (i + 1) * tall] for i in range(fold)])


def solution(mesh):
    grp, gr, gc = (mesh.shape[name] for name in ("grp", "gr", "gc"))
    split = Mesh(mesh.devices.reshape(grp, gr // 2, 2, gc), ("grp", "chip", "core", "gc"))
    rows = ("grp", "chip", "core", "gc")
    in_specs = (P(rows, None, None), P(rows, None, None), P(), P(), P(("chip", "core"), "gc"))
    out_specs = P(("grp", "chip", "core"), "gc")

    def fn(*args):
        return per_device(gr // 2, gc, *args)

    return jax.shard_map(fn, mesh=split, in_specs=in_specs, out_specs=out_specs, check_vma=False)
```

```python
import functools
import math

import jax
import jax.numpy as jnp
from jax import lax
from jax.experimental import pallas as pl
from jax.experimental.pallas import tpu as pltpu
from jax.sharding import Mesh, PartitionSpec as P

PLANE = ("chip", "gc")
CHUNK = 1024
LIMIT = 107 * 2**19
VMEM = pl.BlockSpec(memory_space=pltpu.VMEM)
HBM = pl.BlockSpec(memory_space=pl.ANY)
NT = (((1,), (1,)), ((), ()))


def other_core(value):
    return lax.ppermute(value, "core", [(0, 1), (1, 0)])


def left_parity(chip, col):
    home = col // 2
    return jnp.where(chip < home, col % 2, 1 - col % 2)


def rows_kernel(length, block, cols, act, grad, w_in, w_out, out, act_v, grad_v, in_v, out_v, w_sem, x_sem):
    seqs = out.shape[1]
    rank = w_in.shape[0]
    rows, width = act.shape
    steps = width // CHUNK
    sides = ((act, w_in, act_v, in_v), (grad, w_out, grad_v, out_v))
    copies = []
    for side, (x, w, x_v, w_v) in enumerate(sides):
        for step in range(steps):
            part = pl.ds(step * CHUNK, CHUNK)
            slot = side * steps + step
            pair = (
                pltpu.make_async_copy(w.at[:, part], w_v.at[:, part], w_sem.at[slot]),
                pltpu.make_async_copy(x.at[:, part], x_v.at[:, part], x_sem.at[slot]),
            )
            for copy in pair:
                copy.start()
            copies.append(pair)
    projected = []
    for side, (x, w, x_v, w_v) in enumerate(sides):
        total = jnp.zeros((rows, rank), jnp.float32)
        for step in range(steps):
            for copy in copies[side * steps + step]:
                copy.wait()
            part = pl.ds(step * CHUNK, CHUNK)
            total += lax.dot_general(
                x_v[:, part], w_v[:, part], NT, preferred_element_type=jnp.float32
            )
        projected.append(total)
    both = jnp.concatenate(projected, axis=1).T.astype(out.dtype)
    proj_act, proj_grad = both[:rank], both[rank:]
    many = rank // 2 * seqs
    row = lax.broadcasted_iota(jnp.int32, (many, rank), 0)
    column = lax.broadcasted_iota(jnp.int32, (many, rank), 1)
    token = lax.broadcasted_iota(jnp.int32, (many, rows), 1)
    sequence = lax.broadcasted_iota(jnp.int32, (many, rows), 0) % seqs
    left = []
    for odd in range(2):
        pick = (column == row // seqs * 2 + odd).astype(jnp.float32).astype(out.dtype)
        spread = jnp.dot(pick, proj_grad, preferred_element_type=jnp.float32)
        left.append(jnp.where(token // length == sequence, spread, 0.0).astype(out.dtype))
    nothing = jnp.zeros_like(proj_act)
    right = jnp.concatenate(
        [
            jnp.concatenate([proj_act, nothing], axis=1),
            jnp.concatenate([nothing, proj_act], axis=1),
        ]
    )
    summed = lax.dot_general(
        jnp.concatenate(left, axis=1), right, NT, preferred_element_type=jnp.float32
    )
    summed = summed * (1.0 / math.sqrt(length))
    lanes = 2 * rank
    tiles = block // lanes
    grad_rows = [
        summed[i * seqs : (i + 1) * seqs].astype(out.dtype) for i in range(many // seqs)
    ]
    for place in range(out.shape[0]):
        chip, col = place // cols, place % cols
        odd = col % 2 if chip < col // 2 else 1 - col % 2
        for slot, source in enumerate((2 * chip + odd, col)):
            for i in range(tiles):
                start = slot * block + i * lanes
                out[place, :, start : start + lanes] = grad_rows[source * tiles + i]


def gradient_pieces(plane, cols, block, activations, out_grads, w_in, w_out):
    seqs, length, width = activations.shape
    rank = w_in.shape[0]
    rows = seqs * length
    kind = activations.dtype
    steps = 2 * width // CHUNK
    return pl.pallas_call(
        functools.partial(rows_kernel, length, block, cols),
        out_shape=jax.ShapeDtypeStruct((plane, seqs, 2 * block), kind),
        in_specs=[HBM] * 4,
        out_specs=VMEM,
        scratch_shapes=[
            pltpu.VMEM((rows, width), kind),
            pltpu.VMEM((rows, width), kind),
            pltpu.VMEM((rank, width), kind),
            pltpu.VMEM((rank, width), kind),
            pltpu.SemaphoreType.DMA((steps,)),
            pltpu.SemaphoreType.DMA((steps,)),
        ],
        compiler_params=pltpu.CompilerParams(vmem_limit_bytes=LIMIT),
        cost_estimate=pl.CostEstimate(
            flops=4 * rows * width * rank, bytes_accessed=4 * (rows + rank) * width, transcendentals=0
        ),
        name="gradient_pieces",
    )(activations.reshape(rows, width), out_grads.reshape(rows, width), w_in, w_out)


def precond_kernel(case, got, own, other, out):
    block = own.shape[0]
    tile = min(256, block)
    half = block // 2
    left, right = got.at[:, :block], got.at[:, block:]

    def product(lhs, rhs):
        return jnp.dot(lhs, rhs, preferred_element_type=jnp.float32)

    def whole(pair):
        out[...] = product(left[...], pair[...]).astype(out.dtype)

    def at_home(odd, diagonal, pair):
        for start in range(0, block, tile):
            lanes = slice(start, start + tile)
            total = product(right[:, lanes] * 0.5, diagonal[lanes, lanes])
            if start > 0:
                total += product(right[:, :start], diagonal[:start, lanes])
            if not odd:
                total += product(left[:, :half], pair[:half, lanes])
            elif start + tile > half:
                skip = max(half - start, 0)
                more = product(left[...], pair[:, start + skip : start + tile])
                if skip > 0:
                    more = jnp.concatenate([jnp.zeros((left.shape[0], skip), jnp.float32), more], axis=1)
                total += more
            out[:, lanes] = total.astype(out.dtype)

    branches = [
        functools.partial(whole, own),
        functools.partial(whole, other),
        functools.partial(at_home, False, own, other),
        functools.partial(at_home, False, other, own),
        functools.partial(at_home, True, own, other),
        functools.partial(at_home, True, other, own),
    ]
    for i, branch in enumerate(branches):
        pl.when(case[0] == i)(branch)


def precondition(case, got, own, other):
    rows = got.shape[0]
    block, width = own.shape
    return pl.pallas_call(
        precond_kernel,
        out_shape=jax.ShapeDtypeStruct((rows, width), got.dtype),
        in_specs=[pl.BlockSpec(memory_space=pltpu.SMEM)] + [VMEM] * 3,
        out_specs=VMEM,
        compiler_params=pltpu.CompilerParams(vmem_limit_bytes=16 * 2**20),
        cost_estimate=pl.CostEstimate(
            flops=2 * rows * block * width, bytes_accessed=4 * block * width, transcendentals=0
        ),
        name="precondition",
    )(case, got, own, other)


def terms_kernel(n, fold, scale, core, precond, right, out):
    chips = n // 2
    size = right.shape[0] // n
    step = size // fold

    def packed(terms, row, col):
        lanes = terms[row * size : (row + 1) * size, col * size : (col + 1) * size]
        return jnp.concatenate([lanes[i * step : (i + 1) * step] for i in range(fold)], axis=1)

    def add(first, count):
        held = precond[pl.ds(first * size, count * size), :]
        once = lax.dot_general(held, right[...], NT, preferred_element_type=jnp.float32) * scale
        turned = lax.dot_general(right[...], held, NT, preferred_element_type=jnp.float32) * scale
        for chip in range(count):
            mine = 2 * (first + chip) + core[0]
            for place in range(n):
                out[mine * n + place] += packed(once, chip, place)
                out[place * n + mine] += packed(turned, place, chip)

    out[...] = jnp.zeros_like(out)
    if chips <= 2:
        add(0, chips)
    else:
        pl.loop(0, chips)(functools.partial(add, count=1))


def kernel_terms(n, fold, scale, core, precond, right):
    rows, width = precond.shape
    other = right.shape[0]
    size = other // n
    return pl.pallas_call(
        functools.partial(terms_kernel, n, fold, scale),
        out_shape=jax.ShapeDtypeStruct((n * n, size // fold, fold * size), jnp.float32),
        in_specs=[pl.BlockSpec(memory_space=pltpu.SMEM)] + [VMEM] * 2,
        out_specs=VMEM,
        compiler_params=pltpu.CompilerParams(
            vmem_limit_bytes=max(16 * 2**20, 12 * other * other)
        ),
        cost_estimate=pl.CostEstimate(
            flops=4 * rows * other * width, bytes_accessed=4 * other * other, transcendentals=0
        ),
        name="kernel_terms",
    )(core, precond, right)


def per_device(chips, cols, activations, out_grads, proj_in, proj_out, inv_gram):
    seqs, length, width = activations.shape
    rank = proj_in.shape[1]
    feat = rank * rank
    block = inv_gram.shape[0]
    plane = chips * cols
    half = seqs * plane
    tall = half // chips
    chip, core, col = (lax.axis_index(name) for name in ("chip", "core", "gc"))

    inv_other = other_core(inv_gram)

    pieces = gradient_pieces(plane, cols, block, activations, out_grads, proj_in.T, proj_out.T)
    got = lax.all_to_all(pieces, PLANE, 0, 0, tiled=True).reshape(half, 2 * block)

    mine = got[:, block:]
    theirs = other_core(mine)
    home = col // 2 == chip
    left_other = (left_parity(chip, col) != core).astype(jnp.int32)
    diagonal_other = (col % 2 != core).astype(jnp.int32)
    case = jnp.where(home, 2 + 2 * (col % 2) + diagonal_other, left_other).astype(jnp.int32)
    theirs, precond = lax.optimization_barrier(
        (theirs, precondition(case.reshape(1), got, inv_gram, inv_other))
    )
    mine = mine.reshape(chips, 1, tall, block)
    theirs = theirs.reshape(chips, 1, tall, block)
    right = jnp.where(
        core == 0,
        jnp.concatenate([mine, theirs], axis=1),
        jnp.concatenate([theirs, mine], axis=1),
    ).reshape(2 * half, block)

    fold = max(1, 128 // tall)
    terms = kernel_terms(cols, fold, 8.0 / feat, core.reshape(1).astype(jnp.int32), precond, right)
    total = jnp.sum(lax.all_to_all(terms, ("chip", "core", "gc"), 0, 0, tiled=True), axis=0)
    return jnp.concatenate([total[:, i * tall : (i + 1) * tall] for i in range(fold)])


def solution(mesh):
    grp, gr, gc = (mesh.shape[name] for name in ("grp", "gr", "gc"))
    split = Mesh(mesh.devices.reshape(grp, gr // 2, 2, gc), ("grp", "chip", "core", "gc"))
    rows = ("grp", "chip", "core", "gc")
    in_specs = (P(rows, None, None), P(rows, None, None), P(), P(), P(("chip", "core"), "gc"))
    out_specs = P(("grp", "chip", "core"), "gc")

    def fn(*args):
        return per_device(gr // 2, gc, *args)

    return jax.shard_map(fn, mesh=split, in_specs=in_specs, out_specs=out_specs, check_vma=False)
```

```python
import functools
import math

import jax
import jax.numpy as jnp
from jax import lax
from jax.experimental import pallas as pl
from jax.experimental.pallas import tpu as pltpu
from jax.sharding import Mesh, PartitionSpec as P

PLANE = ("chip", "gc")
CHUNK = 1024
LIMIT = 107 * 2**19
VMEM = pl.BlockSpec(memory_space=pltpu.VMEM)
HBM = pl.BlockSpec(memory_space=pl.ANY)
NT = (((1,), (1,)), ((), ()))


def exchange(value, axes, members):
    order = [i ^ 1 for i in range(members)]
    return lax.all_to_all(value, axes, 0, 0, axis_index_groups=[order], tiled=True)


def other_core(value):
    return lax.ppermute(value, "core", [(0, 1), (1, 0)])


def left_parity(chip, col):
    home = col // 2
    return jnp.where(chip < home, col % 2, 1 - col % 2)


def rows_kernel(length, block, cols, act, grad, w_in, w_out, out, act_v, grad_v, in_v, out_v, w_sem, x_sem):
    seqs = out.shape[1]
    rank = w_in.shape[0]
    rows, width = act.shape
    steps = width // CHUNK
    sides = ((act, w_in, act_v, in_v), (grad, w_out, grad_v, out_v))
    copies = []
    for side, (x, w, x_v, w_v) in enumerate(sides):
        for step in range(steps):
            part = pl.ds(step * CHUNK, CHUNK)
            slot = side * steps + step
            pair = (
                pltpu.make_async_copy(w.at[:, part], w_v.at[:, part], w_sem.at[slot]),
                pltpu.make_async_copy(x.at[:, part], x_v.at[:, part], x_sem.at[slot]),
            )
            for copy in pair:
                copy.start()
            copies.append(pair)
    projected = []
    for side, (x, w, x_v, w_v) in enumerate(sides):
        total = jnp.zeros((rows, rank), jnp.float32)
        for step in range(steps):
            for copy in copies[side * steps + step]:
                copy.wait()
            part = pl.ds(step * CHUNK, CHUNK)
            total += lax.dot_general(
                x_v[:, part], w_v[:, part], NT, preferred_element_type=jnp.float32
            )
        projected.append(total)
    both = jnp.concatenate(projected, axis=1).T.astype(out.dtype)
    proj_act, proj_grad = both[:rank], both[rank:]
    many = rank // 2 * seqs
    row = lax.broadcasted_iota(jnp.int32, (many, rank), 0)
    column = lax.broadcasted_iota(jnp.int32, (many, rank), 1)
    token = lax.broadcasted_iota(jnp.int32, (many, rows), 1)
    sequence = lax.broadcasted_iota(jnp.int32, (many, rows), 0) % seqs
    left = []
    for odd in range(2):
        pick = (column == row // seqs * 2 + odd).astype(jnp.float32).astype(out.dtype)
        spread = jnp.dot(pick, proj_grad, preferred_element_type=jnp.float32)
        left.append(jnp.where(token // length == sequence, spread, 0.0).astype(out.dtype))
    nothing = jnp.zeros_like(proj_act)
    right = jnp.concatenate(
        [
            jnp.concatenate([proj_act, nothing], axis=1),
            jnp.concatenate([nothing, proj_act], axis=1),
        ]
    )
    summed = lax.dot_general(
        jnp.concatenate(left, axis=1), right, NT, preferred_element_type=jnp.float32
    )
    summed = summed * (1.0 / math.sqrt(length))
    lanes = 2 * rank
    tiles = block // lanes
    grad_rows = [
        summed[i * seqs : (i + 1) * seqs].astype(out.dtype) for i in range(many // seqs)
    ]
    for place in range(out.shape[0]):
        chip, col = (place ^ 1) // cols, (place ^ 1) % cols
        odd = col % 2 if chip < col // 2 else 1 - col % 2
        for slot, source in enumerate((2 * chip + odd, col)):
            for i in range(tiles):
                start = slot * block + i * lanes
                out[place, :, start : start + lanes] = grad_rows[source * tiles + i]


def gradient_pieces(plane, cols, block, activations, out_grads, w_in, w_out):
    seqs, length, width = activations.shape
    rank = w_in.shape[0]
    rows = seqs * length
    kind = activations.dtype
    steps = 2 * width // CHUNK
    return pl.pallas_call(
        functools.partial(rows_kernel, length, block, cols),
        out_shape=jax.ShapeDtypeStruct((plane, seqs, 2 * block), kind),
        in_specs=[HBM] * 4,
        out_specs=VMEM,
        scratch_shapes=[
            pltpu.VMEM((rows, width), kind),
            pltpu.VMEM((rows, width), kind),
            pltpu.VMEM((rank, width), kind),
            pltpu.VMEM((rank, width), kind),
            pltpu.SemaphoreType.DMA((steps,)),
            pltpu.SemaphoreType.DMA((steps,)),
        ],
        compiler_params=pltpu.CompilerParams(vmem_limit_bytes=LIMIT),
        cost_estimate=pl.CostEstimate(
            flops=4 * rows * width * rank, bytes_accessed=4 * (rows + rank) * width, transcendentals=0
        ),
        name="gradient_pieces",
    )(activations.reshape(rows, width), out_grads.reshape(rows, width), w_in, w_out)


def precond_kernel(case, got, own, other, out):
    block = own.shape[0]
    tile = min(256, block)
    half = block // 2
    left, right = got.at[:, :block], got.at[:, block:]

    def product(lhs, rhs):
        return jnp.dot(lhs, rhs, preferred_element_type=jnp.float32)

    def whole(pair):
        out[...] = product(left[...], pair[...]).astype(out.dtype)

    def at_home(odd, diagonal, pair):
        for start in range(0, block, tile):
            lanes = slice(start, start + tile)
            total = product(right[:, lanes] * 0.5, diagonal[lanes, lanes])
            if start > 0:
                total += product(right[:, :start], diagonal[:start, lanes])
            if not odd:
                total += product(left[:, :half], pair[:half, lanes])
            elif start + tile > half:
                skip = max(half - start, 0)
                more = product(left[...], pair[:, start + skip : start + tile])
                if skip > 0:
                    more = jnp.concatenate([jnp.zeros((left.shape[0], skip), jnp.float32), more], axis=1)
                total += more
            out[:, lanes] = total.astype(out.dtype)

    branches = [
        functools.partial(whole, own),
        functools.partial(whole, other),
        functools.partial(at_home, False, own, other),
        functools.partial(at_home, False, other, own),
        functools.partial(at_home, True, own, other),
        functools.partial(at_home, True, other, own),
    ]
    for i, branch in enumerate(branches):
        pl.when(case[0] == i)(branch)


def precondition(case, got, own, other):
    rows = got.shape[0]
    block, width = own.shape
    return pl.pallas_call(
        precond_kernel,
        out_shape=jax.ShapeDtypeStruct((rows, width), got.dtype),
        in_specs=[pl.BlockSpec(memory_space=pltpu.SMEM)] + [VMEM] * 3,
        out_specs=VMEM,
        compiler_params=pltpu.CompilerParams(vmem_limit_bytes=16 * 2**20),
        cost_estimate=pl.CostEstimate(
            flops=2 * rows * block * width, bytes_accessed=4 * block * width, transcendentals=0
        ),
        name="precondition",
    )(case, got, own, other)


def terms_kernel(n, fold, scale, core, precond, right, out):
    chips = n // 2
    size = right.shape[0] // n
    step = size // fold

    def packed(terms, row, col):
        lanes = terms[row * size : (row + 1) * size, col * size : (col + 1) * size]
        return jnp.concatenate([lanes[i * step : (i + 1) * step] for i in range(fold)], axis=1)

    def add(first, count):
        held = precond[pl.ds(first * size, count * size), :]
        once = lax.dot_general(held, right[...], NT, preferred_element_type=jnp.float32) * scale
        turned = lax.dot_general(right[...], held, NT, preferred_element_type=jnp.float32) * scale
        for chip in range(count):
            mine, next_to = 2 * (first + chip) + core[0], 2 * (first + chip) + 1 - core[0]
            for place in range(n):
                out[mine * n + (place ^ 1)] += packed(once, chip, place)
                out[place * n + next_to] += packed(turned, place, chip)

    out[...] = jnp.zeros_like(out)
    if chips <= 2:
        add(0, chips)
    else:
        pl.loop(0, chips)(functools.partial(add, count=1))


def kernel_terms(n, fold, scale, core, precond, right):
    rows, width = precond.shape
    other = right.shape[0]
    size = other // n
    return pl.pallas_call(
        functools.partial(terms_kernel, n, fold, scale),
        out_shape=jax.ShapeDtypeStruct((n * n, size // fold, fold * size), jnp.float32),
        in_specs=[pl.BlockSpec(memory_space=pltpu.SMEM)] + [VMEM] * 2,
        out_specs=VMEM,
        compiler_params=pltpu.CompilerParams(
            vmem_limit_bytes=max(16 * 2**20, 12 * other * other)
        ),
        cost_estimate=pl.CostEstimate(
            flops=4 * rows * other * width, bytes_accessed=4 * other * other, transcendentals=0
        ),
        name="kernel_terms",
    )(core, precond, right)


def per_device(chips, cols, activations, out_grads, proj_in, proj_out, inv_gram):
    seqs, length, width = activations.shape
    rank = proj_in.shape[1]
    feat = rank * rank
    block = inv_gram.shape[0]
    plane = chips * cols
    half = seqs * plane
    tall = half // chips
    chip, core, col = (lax.axis_index(name) for name in ("chip", "core", "gc"))

    inv_other = other_core(inv_gram)

    pieces = gradient_pieces(plane, cols, block, activations, out_grads, proj_in.T, proj_out.T)
    got = exchange(pieces, PLANE, plane).reshape(plane // 2, 2, seqs, 2 * block)
    got = jnp.concatenate([got[:, 1:], got[:, :1]], axis=1).reshape(half, 2 * block)

    mine = got[:, block:]
    theirs = other_core(mine)
    home = col // 2 == chip
    left_other = (left_parity(chip, col) != core).astype(jnp.int32)
    diagonal_other = (col % 2 != core).astype(jnp.int32)
    case = jnp.where(home, 2 + 2 * (col % 2) + diagonal_other, left_other).astype(jnp.int32)
    theirs, precond = lax.optimization_barrier(
        (theirs, precondition(case.reshape(1), got, inv_gram, inv_other))
    )
    mine = mine.reshape(chips, 1, tall, block)
    theirs = theirs.reshape(chips, 1, tall, block)
    right = jnp.where(
        core == 0,
        jnp.concatenate([mine, theirs], axis=1),
        jnp.concatenate([theirs, mine], axis=1),
    ).reshape(2 * half, block)

    fold = max(1, 128 // tall)
    terms = kernel_terms(cols, fold, 8.0 / feat, core.reshape(1).astype(jnp.int32), precond, right)
    total = jnp.sum(exchange(terms, ("chip", "core", "gc"), cols * cols), axis=0)
    return jnp.concatenate([total[:, i * tall : (i + 1) * tall] for i in range(fold)])


def solution(mesh):
    grp, gr, gc = (mesh.shape[name] for name in ("grp", "gr", "gc"))
    split = Mesh(mesh.devices.reshape(grp, gr // 2, 2, gc), ("grp", "chip", "core", "gc"))
    rows = ("grp", "chip", "core", "gc")
    in_specs = (P(rows, None, None), P(rows, None, None), P(), P(), P(("chip", "core"), "gc"))
    out_specs = P(("grp", "chip", "core"), "gc")

    def fn(*args):
        return per_device(gr // 2, gc, *args)

    return jax.shard_map(fn, mesh=split, in_specs=in_specs, out_specs=out_specs, check_vma=False)
```

```python
import functools
import math

import jax
import jax.numpy as jnp
from jax import lax
from jax.experimental import pallas as pl
from jax.experimental.pallas import tpu as pltpu
from jax.sharding import Mesh, PartitionSpec as P

PLANE = ("chip", "gc")
CHUNK = 1024
LIMIT = 107 * 2**19
VMEM = pl.BlockSpec(memory_space=pltpu.VMEM)
HBM = pl.BlockSpec(memory_space=pl.ANY)
NT = (((1,), (1,)), ((), ()))


def exchange(value, axes, members, first):
    order = [i ^ first for i in range(members)]
    return lax.all_to_all(value, axes, 0, 0, axis_index_groups=[order], tiled=True)


def leader(chips, cols):
    return chips // 2 * cols + cols // 2


def other_core(value):
    return lax.ppermute(value, "core", [(0, 1), (1, 0)])


def left_parity(chip, col):
    home = col // 2
    return jnp.where(chip < home, col % 2, 1 - col % 2)


def rows_kernel(length, block, cols, act, grad, w_in, w_out, out, act_v, grad_v, in_v, out_v, w_sem, x_sem):
    seqs = out.shape[1]
    rank = w_in.shape[0]
    rows, width = act.shape
    steps = width // CHUNK
    sides = ((act, w_in, act_v, in_v), (grad, w_out, grad_v, out_v))
    copies = []
    for side, (x, w, x_v, w_v) in enumerate(sides):
        for step in range(steps):
            part = pl.ds(step * CHUNK, CHUNK)
            slot = side * steps + step
            pair = (
                pltpu.make_async_copy(w.at[:, part], w_v.at[:, part], w_sem.at[slot]),
                pltpu.make_async_copy(x.at[:, part], x_v.at[:, part], x_sem.at[slot]),
            )
            for copy in pair:
                copy.start()
            copies.append(pair)
    projected = []
    for side, (x, w, x_v, w_v) in enumerate(sides):
        total = jnp.zeros((rows, rank), jnp.float32)
        for step in range(steps):
            for copy in copies[side * steps + step]:
                copy.wait()
            part = pl.ds(step * CHUNK, CHUNK)
            total += lax.dot_general(
                x_v[:, part], w_v[:, part], NT, preferred_element_type=jnp.float32
            )
        projected.append(total)
    both = jnp.concatenate(projected, axis=1).T.astype(out.dtype)
    proj_act, proj_grad = both[:rank], both[rank:]
    many = rank // 2 * seqs
    row = lax.broadcasted_iota(jnp.int32, (many, rank), 0)
    column = lax.broadcasted_iota(jnp.int32, (many, rank), 1)
    token = lax.broadcasted_iota(jnp.int32, (many, rows), 1)
    sequence = lax.broadcasted_iota(jnp.int32, (many, rows), 0) % seqs
    left = []
    for odd in range(2):
        pick = (column == row // seqs * 2 + odd).astype(jnp.float32).astype(out.dtype)
        spread = jnp.dot(pick, proj_grad, preferred_element_type=jnp.float32)
        left.append(jnp.where(token // length == sequence, spread, 0.0).astype(out.dtype))
    nothing = jnp.zeros_like(proj_act)
    right = jnp.concatenate(
        [
            jnp.concatenate([proj_act, nothing], axis=1),
            jnp.concatenate([nothing, proj_act], axis=1),
        ]
    )
    summed = lax.dot_general(
        jnp.concatenate(left, axis=1), right, NT, preferred_element_type=jnp.float32
    )
    summed = summed * (1.0 / math.sqrt(length))
    lanes = 2 * rank
    tiles = block // lanes
    grad_rows = [
        summed[i * seqs : (i + 1) * seqs].astype(out.dtype) for i in range(many // seqs)
    ]
    for place in range(out.shape[0]):
        member = place ^ leader(out.shape[0] // cols, cols)
        chip, col = member // cols, member % cols
        odd = col % 2 if chip < col // 2 else 1 - col % 2
        for slot, source in enumerate((2 * chip + odd, col)):
            for i in range(tiles):
                start = slot * block + i * lanes
                out[place, :, start : start + lanes] = grad_rows[source * tiles + i]


def gradient_pieces(plane, cols, block, activations, out_grads, w_in, w_out):
    seqs, length, width = activations.shape
    rank = w_in.shape[0]
    rows = seqs * length
    kind = activations.dtype
    steps = 2 * width // CHUNK
    return pl.pallas_call(
        functools.partial(rows_kernel, length, block, cols),
        out_shape=jax.ShapeDtypeStruct((plane, seqs, 2 * block), kind),
        in_specs=[HBM] * 4,
        out_specs=VMEM,
        scratch_shapes=[
            pltpu.VMEM((rows, width), kind),
            pltpu.VMEM((rows, width), kind),
            pltpu.VMEM((rank, width), kind),
            pltpu.VMEM((rank, width), kind),
            pltpu.SemaphoreType.DMA((steps,)),
            pltpu.SemaphoreType.DMA((steps,)),
        ],
        compiler_params=pltpu.CompilerParams(vmem_limit_bytes=LIMIT),
        cost_estimate=pl.CostEstimate(
            flops=4 * rows * width * rank, bytes_accessed=4 * (rows + rank) * width, transcendentals=0
        ),
        name="gradient_pieces",
    )(activations.reshape(rows, width), out_grads.reshape(rows, width), w_in, w_out)


def precond_kernel(case, got, own, other, out):
    block = own.shape[0]
    tile = min(256, block)
    half = block // 2
    left, right = got.at[:, :block], got.at[:, block:]

    def product(lhs, rhs):
        return jnp.dot(lhs, rhs, preferred_element_type=jnp.float32)

    def whole(pair):
        out[...] = product(left[...], pair[...]).astype(out.dtype)

    def at_home(odd, diagonal, pair):
        for start in range(0, block, tile):
            lanes = slice(start, start + tile)
            total = product(right[:, lanes] * 0.5, diagonal[lanes, lanes])
            if start > 0:
                total += product(right[:, :start], diagonal[:start, lanes])
            if not odd:
                total += product(left[:, :half], pair[:half, lanes])
            elif start + tile > half:
                skip = max(half - start, 0)
                more = product(left[...], pair[:, start + skip : start + tile])
                if skip > 0:
                    more = jnp.concatenate([jnp.zeros((left.shape[0], skip), jnp.float32), more], axis=1)
                total += more
            out[:, lanes] = total.astype(out.dtype)

    branches = [
        functools.partial(whole, own),
        functools.partial(whole, other),
        functools.partial(at_home, False, own, other),
        functools.partial(at_home, False, other, own),
        functools.partial(at_home, True, own, other),
        functools.partial(at_home, True, other, own),
    ]
    for i, branch in enumerate(branches):
        pl.when(case[0] == i)(branch)


def precondition(case, got, own, other):
    rows = got.shape[0]
    block, width = own.shape
    return pl.pallas_call(
        precond_kernel,
        out_shape=jax.ShapeDtypeStruct((rows, width), got.dtype),
        in_specs=[pl.BlockSpec(memory_space=pltpu.SMEM)] + [VMEM] * 3,
        out_specs=VMEM,
        compiler_params=pltpu.CompilerParams(vmem_limit_bytes=16 * 2**20),
        cost_estimate=pl.CostEstimate(
            flops=2 * rows * block * width, bytes_accessed=4 * block * width, transcendentals=0
        ),
        name="precondition",
    )(case, got, own, other)


def terms_kernel(n, fold, scale, core, precond, right, out):
    chips = n // 2
    size = right.shape[0] // n
    step = size // fold

    def packed(terms, row, col):
        lanes = terms[row * size : (row + 1) * size, col * size : (col + 1) * size]
        return jnp.concatenate([lanes[i * step : (i + 1) * step] for i in range(fold)], axis=1)

    def add(first, count):
        held = precond[pl.ds(first * size, count * size), :]
        once = lax.dot_general(held, right[...], NT, preferred_element_type=jnp.float32) * scale
        turned = lax.dot_general(right[...], held, NT, preferred_element_type=jnp.float32) * scale
        for chip in range(count):
            mine, next_to = 2 * (first + chip) + core[0], 2 * (first + chip) + 1 - core[0]
            for place in range(n):
                out[mine * n + (place ^ 1)] += packed(once, chip, place)
                out[place * n + next_to] += packed(turned, place, chip)

    out[...] = jnp.zeros_like(out)
    if chips <= 2:
        add(0, chips)
    else:
        pl.loop(0, chips)(functools.partial(add, count=1))


def kernel_terms(n, fold, scale, core, precond, right):
    rows, width = precond.shape
    other = right.shape[0]
    size = other // n
    return pl.pallas_call(
        functools.partial(terms_kernel, n, fold, scale),
        out_shape=jax.ShapeDtypeStruct((n * n, size // fold, fold * size), jnp.float32),
        in_specs=[pl.BlockSpec(memory_space=pltpu.SMEM)] + [VMEM] * 2,
        out_specs=VMEM,
        compiler_params=pltpu.CompilerParams(
            vmem_limit_bytes=max(16 * 2**20, 12 * other * other)
        ),
        cost_estimate=pl.CostEstimate(
            flops=4 * rows * other * width, bytes_accessed=4 * other * other, transcendentals=0
        ),
        name="kernel_terms",
    )(core, precond, right)


def per_device(chips, cols, activations, out_grads, proj_in, proj_out, inv_gram):
    seqs, length, width = activations.shape
    rank = proj_in.shape[1]
    feat = rank * rank
    block = inv_gram.shape[0]
    plane = chips * cols
    half = seqs * plane
    tall = half // chips
    chip, core, col = (lax.axis_index(name) for name in ("chip", "core", "gc"))

    inv_other = other_core(inv_gram)

    pieces = gradient_pieces(plane, cols, block, activations, out_grads, proj_in.T, proj_out.T)
    first = leader(chips, cols)
    got = exchange(pieces, PLANE, plane, first)
    got = jnp.concatenate([got[i ^ first] for i in range(plane)])

    mine = got[:, block:]
    theirs = other_core(mine)
    home = col // 2 == chip
    left_other = (left_parity(chip, col) != core).astype(jnp.int32)
    diagonal_other = (col % 2 != core).astype(jnp.int32)
    case = jnp.where(home, 2 + 2 * (col % 2) + diagonal_other, left_other).astype(jnp.int32)
    theirs, precond = lax.optimization_barrier(
        (theirs, precondition(case.reshape(1), got, inv_gram, inv_other))
    )
    mine = mine.reshape(chips, 1, tall, block)
    theirs = theirs.reshape(chips, 1, tall, block)
    right = jnp.where(
        core == 0,
        jnp.concatenate([mine, theirs], axis=1),
        jnp.concatenate([theirs, mine], axis=1),
    ).reshape(2 * half, block)

    fold = max(1, 128 // tall)
    terms = kernel_terms(cols, fold, 8.0 / feat, core.reshape(1).astype(jnp.int32), precond, right)
    total = jnp.sum(exchange(terms, ("chip", "core", "gc"), cols * cols, 1), axis=0)
    return jnp.concatenate([total[:, i * tall : (i + 1) * tall] for i in range(fold)])


def solution(mesh):
    grp, gr, gc = (mesh.shape[name] for name in ("grp", "gr", "gc"))
    split = Mesh(mesh.devices.reshape(grp, gr // 2, 2, gc), ("grp", "chip", "core", "gc"))
    rows = ("grp", "chip", "core", "gc")
    in_specs = (P(rows, None, None), P(rows, None, None), P(), P(), P(("chip", "core"), "gc"))
    out_specs = P(("grp", "chip", "core"), "gc")

    def fn(*args):
        return per_device(gr // 2, gc, *args)

    return jax.shard_map(fn, mesh=split, in_specs=in_specs, out_specs=out_specs, check_vma=False)
```

```python
import functools
import math

import jax
import jax.numpy as jnp
from jax import lax
from jax.experimental import pallas as pl
from jax.experimental.pallas import tpu as pltpu
from jax.sharding import Mesh, PartitionSpec as P

PLANE = ("chip", "gc")
CHUNK = 1024
LIMIT = 107 * 2**19
VMEM = pl.BlockSpec(memory_space=pltpu.VMEM)
HBM = pl.BlockSpec(memory_space=pl.ANY)
NT = (((1,), (1,)), ((), ()))


def exchange(value, axes, members, first):
    order = [i ^ first for i in range(members)]
    return lax.all_to_all(value, axes, 0, 0, axis_index_groups=[order], tiled=True)


def leader(chips, cols):
    return chips // 2 * cols + cols // 2


def other_core(value):
    return lax.ppermute(value, "core", [(0, 1), (1, 0)])


def left_parity(chip, col):
    home = col // 2
    return jnp.where(chip < home, col % 2, 1 - col % 2)


def rows_kernel(length, block, cols, act, grad, w_in, w_out, out, act_v, grad_v, in_v, out_v, w_sem, x_sem):
    seqs = out.shape[1]
    rank = w_in.shape[0]
    rows, width = act.shape
    steps = width // CHUNK
    sides = ((act, w_in, act_v, in_v), (grad, w_out, grad_v, out_v))
    copies = []
    for side, (x, w, x_v, w_v) in enumerate(sides):
        for step in range(steps):
            part = pl.ds(step * CHUNK, CHUNK)
            slot = side * steps + step
            pair = (
                pltpu.make_async_copy(w.at[:, part], w_v.at[:, part], w_sem.at[slot]),
                pltpu.make_async_copy(x.at[:, part], x_v.at[:, part], x_sem.at[slot]),
            )
            for copy in pair:
                copy.start()
            copies.append(pair)
    projected = []
    for side, (x, w, x_v, w_v) in enumerate(sides):
        total = jnp.zeros((rows, rank), jnp.float32)
        for step in range(steps):
            for copy in copies[side * steps + step]:
                copy.wait()
            part = pl.ds(step * CHUNK, CHUNK)
            total += lax.dot_general(
                x_v[:, part], w_v[:, part], NT, preferred_element_type=jnp.float32
            )
        projected.append(total)
    both = jnp.concatenate(projected, axis=1).T.astype(out.dtype)
    proj_act, proj_grad = both[:rank], both[rank:]
    many = rank // 2 * seqs
    row = lax.broadcasted_iota(jnp.int32, (many, rank), 0)
    column = lax.broadcasted_iota(jnp.int32, (many, rank), 1)
    token = lax.broadcasted_iota(jnp.int32, (many, rows), 1)
    sequence = lax.broadcasted_iota(jnp.int32, (many, rows), 0) % seqs
    left = []
    for odd in range(2):
        pick = (column == row // seqs * 2 + odd).astype(jnp.float32).astype(out.dtype)
        spread = jnp.dot(pick, proj_grad, preferred_element_type=jnp.float32)
        left.append(jnp.where(token // length == sequence, spread, 0.0).astype(out.dtype))
    nothing = jnp.zeros_like(proj_act)
    right = jnp.concatenate(
        [
            jnp.concatenate([proj_act, nothing], axis=1),
            jnp.concatenate([nothing, proj_act], axis=1),
        ]
    )
    summed = lax.dot_general(
        jnp.concatenate(left, axis=1), right, NT, preferred_element_type=jnp.float32
    )
    summed = summed * (1.0 / math.sqrt(length))
    lanes = 2 * rank
    tiles = block // lanes
    grad_rows = [
        summed[i * seqs : (i + 1) * seqs].astype(out.dtype) for i in range(many // seqs)
    ]
    for place in range(out.shape[0]):
        member = place ^ leader(out.shape[0] // cols, cols)
        chip, col = member // cols, member % cols
        odd = col % 2 if chip < col // 2 else 1 - col % 2
        for slot, source in enumerate((2 * chip + odd, col)):
            for i in range(tiles):
                start = slot * block + i * lanes
                out[place, :, start : start + lanes] = grad_rows[source * tiles + i]


def gradient_pieces(plane, cols, block, activations, out_grads, w_in, w_out):
    seqs, length, width = activations.shape
    rank = w_in.shape[0]
    rows = seqs * length
    kind = activations.dtype
    steps = 2 * width // CHUNK
    return pl.pallas_call(
        functools.partial(rows_kernel, length, block, cols),
        out_shape=jax.ShapeDtypeStruct((plane, seqs, 2 * block), kind),
        in_specs=[HBM] * 4,
        out_specs=VMEM,
        scratch_shapes=[
            pltpu.VMEM((rows, width), kind),
            pltpu.VMEM((rows, width), kind),
            pltpu.VMEM((rank, width), kind),
            pltpu.VMEM((rank, width), kind),
            pltpu.SemaphoreType.DMA((steps,)),
            pltpu.SemaphoreType.DMA((steps,)),
        ],
        compiler_params=pltpu.CompilerParams(vmem_limit_bytes=LIMIT),
        cost_estimate=pl.CostEstimate(
            flops=4 * rows * width * rank, bytes_accessed=4 * (rows + rank) * width, transcendentals=0
        ),
        name="gradient_pieces",
    )(activations.reshape(rows, width), out_grads.reshape(rows, width), w_in, w_out)


def precond_kernel(case, got, own, other, out):
    block = own.shape[0]
    tile = min(256, block)
    half = block // 2
    left, right = got.at[:, :block], got.at[:, block:]

    def product(lhs, rhs):
        return jnp.dot(lhs, rhs, preferred_element_type=jnp.float32)

    def whole(pair):
        out[...] = product(left[...], pair[...]).astype(out.dtype)

    def at_home(odd, diagonal, pair):
        for start in range(0, block, tile):
            lanes = slice(start, start + tile)
            total = product(right[:, lanes] * 0.5, diagonal[lanes, lanes])
            if start > 0:
                total += product(right[:, :start], diagonal[:start, lanes])
            if not odd:
                total += product(left[:, :half], pair[:half, lanes])
            elif start + tile > half:
                skip = max(half - start, 0)
                more = product(left[...], pair[:, start + skip : start + tile])
                if skip > 0:
                    more = jnp.concatenate([jnp.zeros((left.shape[0], skip), jnp.float32), more], axis=1)
                total += more
            out[:, lanes] = total.astype(out.dtype)

    branches = [
        functools.partial(whole, own),
        functools.partial(whole, other),
        functools.partial(at_home, False, own, other),
        functools.partial(at_home, False, other, own),
        functools.partial(at_home, True, own, other),
        functools.partial(at_home, True, other, own),
    ]
    for i, branch in enumerate(branches):
        pl.when(case[0] == i)(branch)


def precondition(case, got, own, other):
    rows = got.shape[0]
    block, width = own.shape
    return pl.pallas_call(
        precond_kernel,
        out_shape=jax.ShapeDtypeStruct((rows, width), got.dtype),
        in_specs=[pl.BlockSpec(memory_space=pltpu.SMEM)] + [VMEM] * 3,
        out_specs=VMEM,
        compiler_params=pltpu.CompilerParams(vmem_limit_bytes=16 * 2**20),
        cost_estimate=pl.CostEstimate(
            flops=2 * rows * block * width, bytes_accessed=4 * block * width, transcendentals=0
        ),
        name="precondition",
    )(case, got, own, other)


def terms_kernel(n, fold, scale, core, precond, right, out):
    chips = n // 2
    size = right.shape[0] // n
    step = size // fold

    def packed(terms, row, col):
        lanes = terms[row * size : (row + 1) * size, col * size : (col + 1) * size]
        return jnp.concatenate([lanes[i * step : (i + 1) * step] for i in range(fold)], axis=1)

    def add(first, count):
        held = precond[pl.ds(first * size, count * size), :]
        once = lax.dot_general(held, right[...], NT, preferred_element_type=jnp.float32) * scale
        turned = lax.dot_general(right[...], held, NT, preferred_element_type=jnp.float32) * scale
        for chip in range(count):
            mine, next_to = 2 * (first + chip) + core[0], 2 * (first + chip) + 1 - core[0]
            for place in range(n):
                out[mine * n + (place ^ 1)] += packed(once, chip, place)
                out[place * n + next_to] += packed(turned, place, chip)

    out[...] = jnp.zeros_like(out)
    if chips <= 2:
        add(0, chips)
    else:
        pl.loop(0, chips)(functools.partial(add, count=1))


def kernel_terms(n, fold, scale, core, precond, right):
    rows, width = precond.shape
    other = right.shape[0]
    size = other // n
    return pl.pallas_call(
        functools.partial(terms_kernel, n, fold, scale),
        out_shape=jax.ShapeDtypeStruct((n * n, size // fold, fold * size), jnp.float32),
        in_specs=[pl.BlockSpec(memory_space=pltpu.SMEM)] + [VMEM] * 2,
        out_specs=VMEM,
        compiler_params=pltpu.CompilerParams(
            vmem_limit_bytes=max(16 * 2**20, 12 * other * other)
        ),
        cost_estimate=pl.CostEstimate(
            flops=4 * rows * other * width, bytes_accessed=4 * other * other, transcendentals=0
        ),
        name="kernel_terms",
    )(core, precond, right)


def per_device(chips, cols, activations, out_grads, proj_in, proj_out, inv_gram):
    seqs, length, width = activations.shape
    rank = proj_in.shape[1]
    feat = rank * rank
    block = inv_gram.shape[0]
    plane = chips * cols
    half = seqs * plane
    tall = half // chips
    chip, core, col = (lax.axis_index(name) for name in ("chip", "core", "gc"))

    inv_other = other_core(inv_gram)

    pieces = gradient_pieces(plane, cols, block, activations, out_grads, proj_in.T, proj_out.T)
    pieces, inv_other = lax.optimization_barrier((pieces, inv_other))
    first = leader(chips, cols)
    got = exchange(pieces, PLANE, plane, first)
    got = jnp.concatenate([got[i ^ first] for i in range(plane)])

    mine = got[:, block:]
    theirs = other_core(mine)
    home = col // 2 == chip
    left_other = (left_parity(chip, col) != core).astype(jnp.int32)
    diagonal_other = (col % 2 != core).astype(jnp.int32)
    case = jnp.where(home, 2 + 2 * (col % 2) + diagonal_other, left_other).astype(jnp.int32)
    theirs, precond = lax.optimization_barrier(
        (theirs, precondition(case.reshape(1), got, inv_gram, inv_other))
    )
    mine = mine.reshape(chips, 1, tall, block)
    theirs = theirs.reshape(chips, 1, tall, block)
    right = jnp.where(
        core == 0,
        jnp.concatenate([mine, theirs], axis=1),
        jnp.concatenate([theirs, mine], axis=1),
    ).reshape(2 * half, block)

    fold = max(1, 128 // tall)
    terms = kernel_terms(cols, fold, 8.0 / feat, core.reshape(1).astype(jnp.int32), precond, right)
    total = jnp.sum(exchange(terms, ("chip", "core", "gc"), cols * cols, 1), axis=0)
    return jnp.concatenate([total[:, i * tall : (i + 1) * tall] for i in range(fold)])


def solution(mesh):
    grp, gr, gc = (mesh.shape[name] for name in ("grp", "gr", "gc"))
    split = Mesh(mesh.devices.reshape(grp, gr // 2, 2, gc), ("grp", "chip", "core", "gc"))
    rows = ("grp", "chip", "core", "gc")
    in_specs = (P(rows, None, None), P(rows, None, None), P(), P(), P(("chip", "core"), "gc"))
    out_specs = P(("grp", "chip", "core"), "gc")

    def fn(*args):
        return per_device(gr // 2, gc, *args)

    return jax.shard_map(fn, mesh=split, in_specs=in_specs, out_specs=out_specs, check_vma=False)
```

```python
import functools
import math

import jax
import jax.numpy as jnp
from jax import lax
from jax.experimental import pallas as pl
from jax.experimental.pallas import tpu as pltpu
from jax.sharding import Mesh, PartitionSpec as P

PLANE = ("chip", "gc")
CHUNK = 1024
FETCH_LIMIT = 16 * 2**20
LIMIT = 107 * 2**19
VMEM = pl.BlockSpec(memory_space=pltpu.VMEM)
HBM = pl.BlockSpec(memory_space=pl.ANY)
NT = (((1,), (1,)), ((), ()))


def exchange(value, axes, members, first):
    order = [i ^ first for i in range(members)]
    return lax.all_to_all(value, axes, 0, 0, axis_index_groups=[order], tiled=True)


def leader(chips, cols):
    return chips // 2 * cols + cols // 2


def other_core(value):
    return lax.ppermute(value, "core", [(0, 1), (1, 0)])


def left_parity(chip, col):
    home = col // 2
    return jnp.where(chip < home, col % 2, 1 - col % 2)


def rows_kernel(length, block, cols, act, grad, w_in, w_out, out, act_v, grad_v, in_v, out_v, w_sem, x_sem):
    seqs = out.shape[1]
    rank = w_in.shape[0]
    rows, width = act.shape
    steps = width // CHUNK
    sides = ((act, w_in, act_v, in_v), (grad, w_out, grad_v, out_v))
    copies = []
    for side, (x, w, x_v, w_v) in enumerate(sides):
        for step in range(steps):
            part = pl.ds(step * CHUNK, CHUNK)
            slot = side * steps + step
            pair = (
                pltpu.make_async_copy(w.at[:, part], w_v.at[:, part], w_sem.at[slot]),
                pltpu.make_async_copy(x.at[:, part], x_v.at[:, part], x_sem.at[slot]),
            )
            for copy in pair:
                copy.start()
            copies.append(pair)
    projected = []
    for side, (x, w, x_v, w_v) in enumerate(sides):
        total = jnp.zeros((rows, rank), jnp.float32)
        for step in range(steps):
            for copy in copies[side * steps + step]:
                copy.wait()
            part = pl.ds(step * CHUNK, CHUNK)
            total += lax.dot_general(
                x_v[:, part], w_v[:, part], NT, preferred_element_type=jnp.float32
            )
        projected.append(total)
    both = jnp.concatenate(projected, axis=1).T.astype(out.dtype)
    proj_act, proj_grad = both[:rank], both[rank:]
    many = rank // 2 * seqs
    row = lax.broadcasted_iota(jnp.int32, (many, rank), 0)
    column = lax.broadcasted_iota(jnp.int32, (many, rank), 1)
    token = lax.broadcasted_iota(jnp.int32, (many, rows), 1)
    sequence = lax.broadcasted_iota(jnp.int32, (many, rows), 0) % seqs
    left = []
    for odd in range(2):
        pick = (column == row // seqs * 2 + odd).astype(jnp.float32).astype(out.dtype)
        spread = jnp.dot(pick, proj_grad, preferred_element_type=jnp.float32)
        left.append(jnp.where(token // length == sequence, spread, 0.0).astype(out.dtype))
    nothing = jnp.zeros_like(proj_act)
    right = jnp.concatenate(
        [
            jnp.concatenate([proj_act, nothing], axis=1),
            jnp.concatenate([nothing, proj_act], axis=1),
        ]
    )
    summed = lax.dot_general(
        jnp.concatenate(left, axis=1), right, NT, preferred_element_type=jnp.float32
    )
    summed = summed * (1.0 / math.sqrt(length))
    lanes = 2 * rank
    tiles = block // lanes
    grad_rows = [
        summed[i * seqs : (i + 1) * seqs].astype(out.dtype) for i in range(many // seqs)
    ]
    for place in range(out.shape[0]):
        member = place ^ leader(out.shape[0] // cols, cols)
        chip, col = member // cols, member % cols
        odd = col % 2 if chip < col // 2 else 1 - col % 2
        for slot, source in enumerate((2 * chip + odd, col)):
            for i in range(tiles):
                start = slot * block + i * lanes
                out[place, :, start : start + lanes] = grad_rows[source * tiles + i]


def gradient_pieces(plane, cols, block, activations, out_grads, w_in, w_out):
    seqs, length, width = activations.shape
    rank = w_in.shape[0]
    rows = seqs * length
    kind = activations.dtype
    steps = 2 * width // CHUNK
    return pl.pallas_call(
        functools.partial(rows_kernel, length, block, cols),
        out_shape=jax.ShapeDtypeStruct((plane, seqs, 2 * block), kind),
        in_specs=[HBM] * 4,
        out_specs=VMEM,
        scratch_shapes=[
            pltpu.VMEM((rows, width), kind),
            pltpu.VMEM((rows, width), kind),
            pltpu.VMEM((rank, width), kind),
            pltpu.VMEM((rank, width), kind),
            pltpu.SemaphoreType.DMA((steps,)),
            pltpu.SemaphoreType.DMA((steps,)),
        ],
        compiler_params=pltpu.CompilerParams(vmem_limit_bytes=LIMIT),
        cost_estimate=pl.CostEstimate(
            flops=4 * rows * width * rank, bytes_accessed=4 * (rows + rank) * width, transcendentals=0
        ),
        name="gradient_pieces",
    )(activations.reshape(rows, width), out_grads.reshape(rows, width), w_in, w_out)


def fetch_kernel(block, out, sem):
    copy = pltpu.make_async_copy(block, out, sem)
    copy.start()
    copy.wait()


def fetch(block):
    return pl.pallas_call(
        fetch_kernel,
        out_shape=jax.ShapeDtypeStruct(block.shape, block.dtype),
        in_specs=[HBM],
        out_specs=VMEM,
        scratch_shapes=[pltpu.SemaphoreType.DMA],
        compiler_params=pltpu.CompilerParams(vmem_limit_bytes=FETCH_LIMIT),
        cost_estimate=pl.CostEstimate(
            flops=0, bytes_accessed=2 * block.size * block.dtype.itemsize, transcendentals=0
        ),
        name="fetch",
    )(block)


def precond_kernel(case, got, own, other, out):
    block = own.shape[0]
    tile = min(256, block)
    half = block // 2
    left, right = got.at[:, :block], got.at[:, block:]

    def product(lhs, rhs):
        return jnp.dot(lhs, rhs, preferred_element_type=jnp.float32)

    def whole(pair):
        out[...] = product(left[...], pair[...]).astype(out.dtype)

    def at_home(odd, diagonal, pair):
        for start in range(0, block, tile):
            lanes = slice(start, start + tile)
            total = product(right[:, lanes] * 0.5, diagonal[lanes, lanes])
            if start > 0:
                total += product(right[:, :start], diagonal[:start, lanes])
            if not odd:
                total += product(left[:, :half], pair[:half, lanes])
            elif start + tile > half:
                skip = max(half - start, 0)
                more = product(left[...], pair[:, start + skip : start + tile])
                if skip > 0:
                    more = jnp.concatenate([jnp.zeros((left.shape[0], skip), jnp.float32), more], axis=1)
                total += more
            out[:, lanes] = total.astype(out.dtype)

    branches = [
        functools.partial(whole, own),
        functools.partial(whole, other),
        functools.partial(at_home, False, own, other),
        functools.partial(at_home, False, other, own),
        functools.partial(at_home, True, own, other),
        functools.partial(at_home, True, other, own),
    ]
    for i, branch in enumerate(branches):
        pl.when(case[0] == i)(branch)


def precondition(case, got, own, other):
    rows = got.shape[0]
    block, width = own.shape
    return pl.pallas_call(
        precond_kernel,
        out_shape=jax.ShapeDtypeStruct((rows, width), got.dtype),
        in_specs=[pl.BlockSpec(memory_space=pltpu.SMEM)] + [VMEM] * 3,
        out_specs=VMEM,
        compiler_params=pltpu.CompilerParams(vmem_limit_bytes=16 * 2**20),
        cost_estimate=pl.CostEstimate(
            flops=2 * rows * block * width, bytes_accessed=4 * block * width, transcendentals=0
        ),
        name="precondition",
    )(case, got, own, other)


def terms_kernel(n, fold, scale, core, precond, right, out):
    chips = n // 2
    size = right.shape[0] // n
    step = size // fold

    def packed(terms, row, col):
        lanes = terms[row * size : (row + 1) * size, col * size : (col + 1) * size]
        return jnp.concatenate([lanes[i * step : (i + 1) * step] for i in range(fold)], axis=1)

    def add(first, count):
        held = precond[pl.ds(first * size, count * size), :]
        once = lax.dot_general(held, right[...], NT, preferred_element_type=jnp.float32) * scale
        turned = lax.dot_general(right[...], held, NT, preferred_element_type=jnp.float32) * scale
        for chip in range(count):
            mine, next_to = 2 * (first + chip) + core[0], 2 * (first + chip) + 1 - core[0]
            for place in range(n):
                out[mine * n + (place ^ 1)] += packed(once, chip, place)
                out[place * n + next_to] += packed(turned, place, chip)

    out[...] = jnp.zeros_like(out)
    if chips <= 2:
        add(0, chips)
    else:
        pl.loop(0, chips)(functools.partial(add, count=1))


def kernel_terms(n, fold, scale, core, precond, right):
    rows, width = precond.shape
    other = right.shape[0]
    size = other // n
    return pl.pallas_call(
        functools.partial(terms_kernel, n, fold, scale),
        out_shape=jax.ShapeDtypeStruct((n * n, size // fold, fold * size), jnp.float32),
        in_specs=[pl.BlockSpec(memory_space=pltpu.SMEM)] + [VMEM] * 2,
        out_specs=VMEM,
        compiler_params=pltpu.CompilerParams(
            vmem_limit_bytes=max(16 * 2**20, 12 * other * other)
        ),
        cost_estimate=pl.CostEstimate(
            flops=4 * rows * other * width, bytes_accessed=4 * other * other, transcendentals=0
        ),
        name="kernel_terms",
    )(core, precond, right)


def per_device(chips, cols, activations, out_grads, proj_in, proj_out, inv_gram):
    seqs, length, width = activations.shape
    rank = proj_in.shape[1]
    feat = rank * rank
    block = inv_gram.shape[0]
    plane = chips * cols
    half = seqs * plane
    tall = half // chips
    chip, core, col = (lax.axis_index(name) for name in ("chip", "core", "gc"))

    inv_other = other_core(inv_gram)

    pieces = gradient_pieces(plane, cols, block, activations, out_grads, proj_in.T, proj_out.T)
    pieces, inv_other = lax.optimization_barrier((pieces, inv_other))
    inv_other = fetch(inv_other)
    first = leader(chips, cols)
    got = exchange(pieces, PLANE, plane, first)
    got = jnp.concatenate([got[i ^ first] for i in range(plane)])

    mine = got[:, block:]
    theirs = other_core(mine)
    home = col // 2 == chip
    left_other = (left_parity(chip, col) != core).astype(jnp.int32)
    diagonal_other = (col % 2 != core).astype(jnp.int32)
    case = jnp.where(home, 2 + 2 * (col % 2) + diagonal_other, left_other).astype(jnp.int32)
    theirs, precond = lax.optimization_barrier(
        (theirs, precondition(case.reshape(1), got, inv_gram, inv_other))
    )
    mine = mine.reshape(chips, 1, tall, block)
    theirs = theirs.reshape(chips, 1, tall, block)
    right = jnp.where(
        core == 0,
        jnp.concatenate([mine, theirs], axis=1),
        jnp.concatenate([theirs, mine], axis=1),
    ).reshape(2 * half, block)

    fold = max(1, 128 // tall)
    terms = kernel_terms(cols, fold, 8.0 / feat, core.reshape(1).astype(jnp.int32), precond, right)
    total = jnp.sum(exchange(terms, ("chip", "core", "gc"), cols * cols, 1), axis=0)
    return jnp.concatenate([total[:, i * tall : (i + 1) * tall] for i in range(fold)])


def solution(mesh):
    grp, gr, gc = (mesh.shape[name] for name in ("grp", "gr", "gc"))
    split = Mesh(mesh.devices.reshape(grp, gr // 2, 2, gc), ("grp", "chip", "core", "gc"))
    rows = ("grp", "chip", "core", "gc")
    in_specs = (P(rows, None, None), P(rows, None, None), P(), P(), P(("chip", "core"), "gc"))
    out_specs = P(("grp", "chip", "core"), "gc")

    def fn(*args):
        return per_device(gr // 2, gc, *args)

    return jax.shard_map(fn, mesh=split, in_specs=in_specs, out_specs=out_specs, check_vma=False)
```

```python
import functools
import math

import jax
import jax.numpy as jnp
from jax import lax
from jax.experimental import pallas as pl
from jax.experimental.pallas import tpu as pltpu
from jax.sharding import Mesh, PartitionSpec as P

PLANE = ("chip", "gc")
CHUNK = 1024
FETCH_LIMIT = 16 * 2**20
LIMIT = 107 * 2**19
VMEM = pl.BlockSpec(memory_space=pltpu.VMEM)
HBM = pl.BlockSpec(memory_space=pl.ANY)
NT = (((1,), (1,)), ((), ()))


def exchange(value, axes, members, first):
    order = [i ^ first for i in range(members)]
    return lax.all_to_all(value, axes, 0, 0, axis_index_groups=[order], tiled=True)


def leader(chips, cols):
    return chips // 2 * cols + cols // 2


def other_core(value):
    return lax.ppermute(value, "core", [(0, 1), (1, 0)])


def left_parity(chip, col):
    home = col // 2
    return jnp.where(chip < home, col % 2, 1 - col % 2)


def rows_kernel(length, block, cols, act, grad, w_in, w_out, out, act_v, grad_v, in_v, out_v, w_sem, x_sem):
    seqs = out.shape[1]
    rank = w_in.shape[0]
    rows, width = act.shape
    steps = width // CHUNK
    sides = ((act, w_in, act_v, in_v), (grad, w_out, grad_v, out_v))
    copies = []
    for side, (x, w, x_v, w_v) in enumerate(sides):
        for step in range(steps):
            part = pl.ds(step * CHUNK, CHUNK)
            slot = side * steps + step
            pair = (
                pltpu.make_async_copy(w.at[:, part], w_v.at[:, part], w_sem.at[slot]),
                pltpu.make_async_copy(x.at[:, part], x_v.at[:, part], x_sem.at[slot]),
            )
            for copy in pair:
                copy.start()
            copies.append(pair)
    projected = []
    for side, (x, w, x_v, w_v) in enumerate(sides):
        total = jnp.zeros((rows, rank), jnp.float32)
        for step in range(steps):
            for copy in copies[side * steps + step]:
                copy.wait()
            part = pl.ds(step * CHUNK, CHUNK)
            total += lax.dot_general(
                x_v[:, part], w_v[:, part], NT, preferred_element_type=jnp.float32
            )
        projected.append(total)
    both = jnp.concatenate(projected, axis=1).T.astype(out.dtype)
    proj_act, proj_grad = both[:rank], both[rank:]
    many = rank // 2 * seqs
    row = lax.broadcasted_iota(jnp.int32, (many, rank), 0)
    column = lax.broadcasted_iota(jnp.int32, (many, rank), 1)
    token = lax.broadcasted_iota(jnp.int32, (many, rows), 1)
    sequence = lax.broadcasted_iota(jnp.int32, (many, rows), 0) % seqs
    left = []
    for odd in range(2):
        pick = (column == row // seqs * 2 + odd).astype(jnp.float32).astype(out.dtype)
        spread = jnp.dot(pick, proj_grad, preferred_element_type=jnp.float32)
        left.append(jnp.where(token // length == sequence, spread, 0.0).astype(out.dtype))
    nothing = jnp.zeros_like(proj_act)
    right = jnp.concatenate(
        [
            jnp.concatenate([proj_act, nothing], axis=1),
            jnp.concatenate([nothing, proj_act], axis=1),
        ]
    )
    summed = lax.dot_general(
        jnp.concatenate(left, axis=1), right, NT, preferred_element_type=jnp.float32
    )
    summed = summed * (1.0 / math.sqrt(length))
    lanes = 2 * rank
    tiles = block // lanes
    grad_rows = [
        summed[i * seqs : (i + 1) * seqs].astype(out.dtype) for i in range(many // seqs)
    ]
    for place in range(out.shape[0]):
        member = place ^ leader(out.shape[0] // cols, cols)
        chip, col = member // cols, member % cols
        odd = col % 2 if chip < col // 2 else 1 - col % 2
        for slot, source in enumerate((2 * chip + odd, col)):
            for i in range(tiles):
                start = slot * block + i * lanes
                out[place, :, start : start + lanes] = grad_rows[source * tiles + i]


def gradient_pieces(plane, cols, block, activations, out_grads, w_in, w_out):
    seqs, length, width = activations.shape
    rank = w_in.shape[0]
    rows = seqs * length
    kind = activations.dtype
    steps = 2 * width // CHUNK
    return pl.pallas_call(
        functools.partial(rows_kernel, length, block, cols),
        out_shape=jax.ShapeDtypeStruct((plane, seqs, 2 * block), kind),
        in_specs=[HBM] * 4,
        out_specs=VMEM,
        scratch_shapes=[
            pltpu.VMEM((rows, width), kind),
            pltpu.VMEM((rows, width), kind),
            pltpu.VMEM((rank, width), kind),
            pltpu.VMEM((rank, width), kind),
            pltpu.SemaphoreType.DMA((steps,)),
            pltpu.SemaphoreType.DMA((steps,)),
        ],
        compiler_params=pltpu.CompilerParams(vmem_limit_bytes=LIMIT),
        cost_estimate=pl.CostEstimate(
            flops=4 * rows * width * rank, bytes_accessed=4 * (rows + rank) * width, transcendentals=0
        ),
        name="gradient_pieces",
    )(activations.reshape(rows, width), out_grads.reshape(rows, width), w_in, w_out)


def fetch_kernel(own, other, own_v, other_v, sem):
    copies = [
        pltpu.make_async_copy(own, own_v, sem.at[0]),
        pltpu.make_async_copy(other, other_v, sem.at[1]),
    ]
    for copy in copies:
        copy.start()
    for copy in copies:
        copy.wait()


def fetch(own, other):
    return pl.pallas_call(
        fetch_kernel,
        out_shape=[jax.ShapeDtypeStruct(own.shape, own.dtype)] * 2,
        in_specs=[HBM] * 2,
        out_specs=[VMEM] * 2,
        scratch_shapes=[pltpu.SemaphoreType.DMA((2,))],
        compiler_params=pltpu.CompilerParams(vmem_limit_bytes=FETCH_LIMIT),
        cost_estimate=pl.CostEstimate(
            flops=0, bytes_accessed=4 * own.size * own.dtype.itemsize, transcendentals=0
        ),
        name="fetch",
    )(own, other)


def precond_kernel(case, got, own, other, out):
    block = own.shape[0]
    tile = min(256, block)
    half = block // 2
    left, right = got.at[:, :block], got.at[:, block:]

    def product(lhs, rhs):
        return jnp.dot(lhs, rhs, preferred_element_type=jnp.float32)

    def whole(pair):
        out[...] = product(left[...], pair[...]).astype(out.dtype)

    def at_home(odd, diagonal, pair):
        for start in range(0, block, tile):
            lanes = slice(start, start + tile)
            total = product(right[:, lanes] * 0.5, diagonal[lanes, lanes])
            if start > 0:
                total += product(right[:, :start], diagonal[:start, lanes])
            if not odd:
                total += product(left[:, :half], pair[:half, lanes])
            elif start + tile > half:
                skip = max(half - start, 0)
                more = product(left[...], pair[:, start + skip : start + tile])
                if skip > 0:
                    more = jnp.concatenate([jnp.zeros((left.shape[0], skip), jnp.float32), more], axis=1)
                total += more
            out[:, lanes] = total.astype(out.dtype)

    branches = [
        functools.partial(whole, own),
        functools.partial(whole, other),
        functools.partial(at_home, False, own, other),
        functools.partial(at_home, False, other, own),
        functools.partial(at_home, True, own, other),
        functools.partial(at_home, True, other, own),
    ]
    for i, branch in enumerate(branches):
        pl.when(case[0] == i)(branch)


def precondition(case, got, own, other):
    rows = got.shape[0]
    block, width = own.shape
    return pl.pallas_call(
        precond_kernel,
        out_shape=jax.ShapeDtypeStruct((rows, width), got.dtype),
        in_specs=[pl.BlockSpec(memory_space=pltpu.SMEM)] + [VMEM] * 3,
        out_specs=VMEM,
        compiler_params=pltpu.CompilerParams(vmem_limit_bytes=16 * 2**20),
        cost_estimate=pl.CostEstimate(
            flops=2 * rows * block * width, bytes_accessed=4 * block * width, transcendentals=0
        ),
        name="precondition",
    )(case, got, own, other)


def terms_kernel(n, fold, scale, core, precond, right, out):
    chips = n // 2
    size = right.shape[0] // n
    step = size // fold

    def packed(terms, row, col):
        lanes = terms[row * size : (row + 1) * size, col * size : (col + 1) * size]
        return jnp.concatenate([lanes[i * step : (i + 1) * step] for i in range(fold)], axis=1)

    def add(first, count):
        held = precond[pl.ds(first * size, count * size), :]
        once = lax.dot_general(held, right[...], NT, preferred_element_type=jnp.float32) * scale
        turned = lax.dot_general(right[...], held, NT, preferred_element_type=jnp.float32) * scale
        for chip in range(count):
            mine, next_to = 2 * (first + chip) + core[0], 2 * (first + chip) + 1 - core[0]
            for place in range(n):
                out[mine * n + (place ^ 1)] += packed(once, chip, place)
                out[place * n + next_to] += packed(turned, place, chip)

    out[...] = jnp.zeros_like(out)
    if chips <= 2:
        add(0, chips)
    else:
        pl.loop(0, chips)(functools.partial(add, count=1))


def kernel_terms(n, fold, scale, core, precond, right):
    rows, width = precond.shape
    other = right.shape[0]
    size = other // n
    return pl.pallas_call(
        functools.partial(terms_kernel, n, fold, scale),
        out_shape=jax.ShapeDtypeStruct((n * n, size // fold, fold * size), jnp.float32),
        in_specs=[pl.BlockSpec(memory_space=pltpu.SMEM)] + [VMEM] * 2,
        out_specs=VMEM,
        compiler_params=pltpu.CompilerParams(
            vmem_limit_bytes=max(16 * 2**20, 12 * other * other)
        ),
        cost_estimate=pl.CostEstimate(
            flops=4 * rows * other * width, bytes_accessed=4 * other * other, transcendentals=0
        ),
        name="kernel_terms",
    )(core, precond, right)


def per_device(chips, cols, activations, out_grads, proj_in, proj_out, inv_gram):
    seqs, length, width = activations.shape
    rank = proj_in.shape[1]
    feat = rank * rank
    block = inv_gram.shape[0]
    plane = chips * cols
    half = seqs * plane
    tall = half // chips
    chip, core, col = (lax.axis_index(name) for name in ("chip", "core", "gc"))

    inv_other = other_core(inv_gram)

    pieces = gradient_pieces(plane, cols, block, activations, out_grads, proj_in.T, proj_out.T)
    pieces, inv_other = lax.optimization_barrier((pieces, inv_other))
    inv_own, inv_other = fetch(inv_gram, inv_other)
    first = leader(chips, cols)
    got = exchange(pieces, PLANE, plane, first)
    got = jnp.concatenate([got[i ^ first] for i in range(plane)])

    mine = got[:, block:]
    theirs = other_core(mine)
    home = col // 2 == chip
    left_other = (left_parity(chip, col) != core).astype(jnp.int32)
    diagonal_other = (col % 2 != core).astype(jnp.int32)
    case = jnp.where(home, 2 + 2 * (col % 2) + diagonal_other, left_other).astype(jnp.int32)
    theirs, precond = lax.optimization_barrier(
        (theirs, precondition(case.reshape(1), got, inv_own, inv_other))
    )
    mine = mine.reshape(chips, 1, tall, block)
    theirs = theirs.reshape(chips, 1, tall, block)
    right = jnp.where(
        core == 0,
        jnp.concatenate([mine, theirs], axis=1),
        jnp.concatenate([theirs, mine], axis=1),
    ).reshape(2 * half, block)

    fold = max(1, 128 // tall)
    terms = kernel_terms(cols, fold, 8.0 / feat, core.reshape(1).astype(jnp.int32), precond, right)
    total = jnp.sum(exchange(terms, ("chip", "core", "gc"), cols * cols, 1), axis=0)
    return jnp.concatenate([total[:, i * tall : (i + 1) * tall] for i in range(fold)])


def solution(mesh):
    grp, gr, gc = (mesh.shape[name] for name in ("grp", "gr", "gc"))
    split = Mesh(mesh.devices.reshape(grp, gr // 2, 2, gc), ("grp", "chip", "core", "gc"))
    rows = ("grp", "chip", "core", "gc")
    in_specs = (P(rows, None, None), P(rows, None, None), P(), P(), P(("chip", "core"), "gc"))
    out_specs = P(("grp", "chip", "core"), "gc")

    def fn(*args):
        return per_device(gr // 2, gc, *args)

    return jax.shard_map(fn, mesh=split, in_specs=in_specs, out_specs=out_specs, check_vma=False)
```

```python
import functools
import math

import jax
import jax.numpy as jnp
from jax import lax
from jax.experimental import pallas as pl
from jax.experimental.pallas import tpu as pltpu
from jax.sharding import Mesh, PartitionSpec as P

PLANE = ("chip", "gc")
CHUNK = 1024
FETCH_LIMIT = 16 * 2**20
LIMIT = 107 * 2**19
VMEM = pl.BlockSpec(memory_space=pltpu.VMEM)
HBM = pl.BlockSpec(memory_space=pl.ANY)
NT = (((1,), (1,)), ((), ()))


def exchange(value, axes, members, first):
    order = [i ^ first for i in range(members)]
    return lax.all_to_all(value, axes, 0, 0, axis_index_groups=[order], tiled=True)


def leader(chips, cols):
    return chips // 2 * cols + cols // 2


def other_core(value):
    return lax.ppermute(value, "core", [(0, 1), (1, 0)])


def left_parity(chip, col):
    home = col // 2
    return jnp.where(chip < home, col % 2, 1 - col % 2)


def rows_kernel(length, block, cols, act, grad, w_in, w_out, out, act_v, grad_v, in_v, out_v, w_sem, x_sem):
    seqs = out.shape[1]
    rank = w_in.shape[0]
    rows, width = act.shape
    steps = width // CHUNK
    sides = ((act, w_in, act_v, in_v), (grad, w_out, grad_v, out_v))
    copies = []
    for side, (x, w, x_v, w_v) in enumerate(sides):
        for step in range(steps):
            part = pl.ds(step * CHUNK, CHUNK)
            slot = side * steps + step
            pair = (
                pltpu.make_async_copy(w.at[:, part], w_v.at[:, part], w_sem.at[slot]),
                pltpu.make_async_copy(x.at[:, part], x_v.at[:, part], x_sem.at[slot]),
            )
            for copy in pair:
                copy.start()
            copies.append(pair)
    projected = []
    for side, (x, w, x_v, w_v) in enumerate(sides):
        total = jnp.zeros((rows, rank), jnp.float32)
        for step in range(steps):
            for copy in copies[side * steps + step]:
                copy.wait()
            part = pl.ds(step * CHUNK, CHUNK)
            total += lax.dot_general(
                x_v[:, part], w_v[:, part], NT, preferred_element_type=jnp.float32
            )
        projected.append(total)
    both = jnp.concatenate(projected, axis=1).T.astype(out.dtype)
    proj_act, proj_grad = both[:rank], both[rank:]
    many = rank // 2 * seqs
    row = lax.broadcasted_iota(jnp.int32, (many, rank), 0)
    column = lax.broadcasted_iota(jnp.int32, (many, rank), 1)
    token = lax.broadcasted_iota(jnp.int32, (many, rows), 1)
    sequence = lax.broadcasted_iota(jnp.int32, (many, rows), 0) % seqs
    left = []
    for odd in range(2):
        pick = (column == row // seqs * 2 + odd).astype(jnp.float32).astype(out.dtype)
        spread = jnp.dot(pick, proj_grad, preferred_element_type=jnp.float32)
        left.append(jnp.where(token // length == sequence, spread, 0.0).astype(out.dtype))
    nothing = jnp.zeros_like(proj_act)
    right = jnp.concatenate(
        [
            jnp.concatenate([proj_act, nothing], axis=1),
            jnp.concatenate([nothing, proj_act], axis=1),
        ]
    )
    summed = lax.dot_general(
        jnp.concatenate(left, axis=1), right, NT, preferred_element_type=jnp.float32
    )
    summed = summed * (1.0 / math.sqrt(length))
    lanes = 2 * rank
    tiles = block // lanes
    grad_rows = [
        summed[i * seqs : (i + 1) * seqs].astype(out.dtype) for i in range(many // seqs)
    ]
    for place in range(out.shape[0]):
        member = place ^ leader(out.shape[0] // cols, cols)
        chip, col = member // cols, member % cols
        odd = col % 2 if chip < col // 2 else 1 - col % 2
        for slot, source in enumerate((2 * chip + odd, col)):
            for i in range(tiles):
                start = slot * block + i * lanes
                out[place, :, start : start + lanes] = grad_rows[source * tiles + i]


def gradient_pieces(plane, cols, block, activations, out_grads, w_in, w_out):
    seqs, length, width = activations.shape
    rank = w_in.shape[0]
    rows = seqs * length
    kind = activations.dtype
    steps = 2 * width // CHUNK
    return pl.pallas_call(
        functools.partial(rows_kernel, length, block, cols),
        out_shape=jax.ShapeDtypeStruct((plane, seqs, 2 * block), kind),
        in_specs=[HBM] * 4,
        out_specs=VMEM,
        scratch_shapes=[
            pltpu.VMEM((rows, width), kind),
            pltpu.VMEM((rows, width), kind),
            pltpu.VMEM((rank, width), kind),
            pltpu.VMEM((rank, width), kind),
            pltpu.SemaphoreType.DMA((steps,)),
            pltpu.SemaphoreType.DMA((steps,)),
        ],
        compiler_params=pltpu.CompilerParams(vmem_limit_bytes=LIMIT),
        cost_estimate=pl.CostEstimate(
            flops=4 * rows * width * rank, bytes_accessed=4 * (rows + rank) * width, transcendentals=0
        ),
        name="gradient_pieces",
    )(activations.reshape(rows, width), out_grads.reshape(rows, width), w_in, w_out)


def fetch_kernel(block, out, sem):
    copy = pltpu.make_async_copy(block, out, sem)
    copy.start()
    copy.wait()


def fetch(block):
    return pl.pallas_call(
        fetch_kernel,
        out_shape=jax.ShapeDtypeStruct(block.shape, block.dtype),
        in_specs=[HBM],
        out_specs=VMEM,
        scratch_shapes=[pltpu.SemaphoreType.DMA],
        compiler_params=pltpu.CompilerParams(vmem_limit_bytes=FETCH_LIMIT),
        cost_estimate=pl.CostEstimate(
            flops=0, bytes_accessed=2 * block.size * block.dtype.itemsize, transcendentals=0
        ),
        name="fetch",
    )(block)


def precond_kernel(case, got, own, other, out):
    block = own.shape[0]
    tile = min(256, block)
    half = block // 2
    left, right = got.at[:, :block], got.at[:, block:]

    def product(lhs, rhs):
        return jnp.dot(lhs, rhs, preferred_element_type=jnp.float32)

    def whole(pair):
        out[...] = product(left[...], pair[...]).astype(out.dtype)

    def at_home(odd, diagonal, pair):
        for start in range(0, block, tile):
            lanes = slice(start, start + tile)
            total = product(right[:, lanes] * 0.5, diagonal[lanes, lanes])
            if start > 0:
                total += product(right[:, :start], diagonal[:start, lanes])
            if not odd:
                total += product(left[:, :half], pair[:half, lanes])
            elif start + tile > half:
                skip = max(half - start, 0)
                more = product(left[...], pair[:, start + skip : start + tile])
                if skip > 0:
                    more = jnp.concatenate([jnp.zeros((left.shape[0], skip), jnp.float32), more], axis=1)
                total += more
            out[:, lanes] = total.astype(out.dtype)

    branches = [
        functools.partial(whole, own),
        functools.partial(whole, other),
        functools.partial(at_home, False, own, other),
        functools.partial(at_home, False, other, own),
        functools.partial(at_home, True, own, other),
        functools.partial(at_home, True, other, own),
    ]
    for i, branch in enumerate(branches):
        pl.when(case[0] == i)(branch)


def precondition(case, got, own, other):
    rows = got.shape[0]
    block, width = own.shape
    return pl.pallas_call(
        precond_kernel,
        out_shape=jax.ShapeDtypeStruct((rows, width), got.dtype),
        in_specs=[pl.BlockSpec(memory_space=pltpu.SMEM)] + [VMEM] * 3,
        out_specs=VMEM,
        compiler_params=pltpu.CompilerParams(vmem_limit_bytes=16 * 2**20),
        cost_estimate=pl.CostEstimate(
            flops=2 * rows * block * width, bytes_accessed=4 * block * width, transcendentals=0
        ),
        name="precondition",
    )(case, got, own, other)


def terms_kernel(n, fold, scale, core, precond, right, out):
    chips = n // 2
    size = right.shape[0] // n
    step = size // fold

    def packed(terms, row, col):
        lanes = terms[row * size : (row + 1) * size, col * size : (col + 1) * size]
        return jnp.concatenate([lanes[i * step : (i + 1) * step] for i in range(fold)], axis=1)

    def add(first, count):
        held = precond[pl.ds(first * size, count * size), :]
        once = lax.dot_general(held, right[...], NT, preferred_element_type=jnp.float32) * scale
        turned = lax.dot_general(right[...], held, NT, preferred_element_type=jnp.float32) * scale
        for chip in range(count):
            mine = 2 * (first + chip) + core[0]
            across = ((2 * (first + chip)) ^ (n // 2)) + core[0]
            for place in range(n):
                out[mine * n + (place ^ (n // 2))] += packed(once, chip, place)
                out[place * n + across] += packed(turned, place, chip)

    out[...] = jnp.zeros_like(out)
    if chips <= 2:
        add(0, chips)
    else:
        pl.loop(0, chips)(functools.partial(add, count=1))


def kernel_terms(n, fold, scale, core, precond, right):
    rows, width = precond.shape
    other = right.shape[0]
    size = other // n
    return pl.pallas_call(
        functools.partial(terms_kernel, n, fold, scale),
        out_shape=jax.ShapeDtypeStruct((n * n, size // fold, fold * size), jnp.float32),
        in_specs=[pl.BlockSpec(memory_space=pltpu.SMEM)] + [VMEM] * 2,
        out_specs=VMEM,
        compiler_params=pltpu.CompilerParams(
            vmem_limit_bytes=max(16 * 2**20, 12 * other * other)
        ),
        cost_estimate=pl.CostEstimate(
            flops=4 * rows * other * width, bytes_accessed=4 * other * other, transcendentals=0
        ),
        name="kernel_terms",
    )(core, precond, right)


def per_device(chips, cols, activations, out_grads, proj_in, proj_out, inv_gram):
    seqs, length, width = activations.shape
    rank = proj_in.shape[1]
    feat = rank * rank
    block = inv_gram.shape[0]
    plane = chips * cols
    half = seqs * plane
    tall = half // chips
    chip, core, col = (lax.axis_index(name) for name in ("chip", "core", "gc"))

    inv_other = other_core(inv_gram)

    pieces = gradient_pieces(plane, cols, block, activations, out_grads, proj_in.T, proj_out.T)
    pieces, inv_other = lax.optimization_barrier((pieces, inv_other))
    inv_other = fetch(inv_other)
    first = leader(chips, cols)
    got = exchange(pieces, PLANE, plane, first)
    got = jnp.concatenate([got[i ^ first] for i in range(plane)])

    mine = got[:, block:]
    theirs = other_core(mine)
    home = col // 2 == chip
    left_other = (left_parity(chip, col) != core).astype(jnp.int32)
    diagonal_other = (col % 2 != core).astype(jnp.int32)
    case = jnp.where(home, 2 + 2 * (col % 2) + diagonal_other, left_other).astype(jnp.int32)
    theirs, precond = lax.optimization_barrier(
        (theirs, precondition(case.reshape(1), got, inv_gram, inv_other))
    )
    mine = mine.reshape(chips, 1, tall, block)
    theirs = theirs.reshape(chips, 1, tall, block)
    right = jnp.where(
        core == 0,
        jnp.concatenate([mine, theirs], axis=1),
        jnp.concatenate([theirs, mine], axis=1),
    ).reshape(2 * half, block)

    fold = max(1, 128 // tall)
    terms = kernel_terms(cols, fold, 8.0 / feat, core.reshape(1).astype(jnp.int32), precond, right)
    total = jnp.sum(exchange(terms, ("chip", "core", "gc"), cols * cols, cols // 2), axis=0)
    return jnp.concatenate([total[:, i * tall : (i + 1) * tall] for i in range(fold)])


def solution(mesh):
    grp, gr, gc = (mesh.shape[name] for name in ("grp", "gr", "gc"))
    split = Mesh(mesh.devices.reshape(grp, gr // 2, 2, gc), ("grp", "chip", "core", "gc"))
    rows = ("grp", "chip", "core", "gc")
    in_specs = (P(rows, None, None), P(rows, None, None), P(), P(), P(("chip", "core"), "gc"))
    out_specs = P(("grp", "chip", "core"), "gc")

    def fn(*args):
        return per_device(gr // 2, gc, *args)

    return jax.shard_map(fn, mesh=split, in_specs=in_specs, out_specs=out_specs, check_vma=False)
```

```python
import functools
import math

import jax
import jax.numpy as jnp
from jax import lax
from jax.experimental import pallas as pl
from jax.experimental.pallas import tpu as pltpu
from jax.sharding import Mesh, PartitionSpec as P

PLANE = ("chip", "gc")
CHUNK = 1024
FETCH_LIMIT = 16 * 2**20
LIMIT = 107 * 2**19
VMEM = pl.BlockSpec(memory_space=pltpu.VMEM)
HBM = pl.BlockSpec(memory_space=pl.ANY)
NT = (((1,), (1,)), ((), ()))


def exchange(value, axes, members, first):
    order = [i ^ first for i in range(members)]
    return lax.all_to_all(value, axes, 0, 0, axis_index_groups=[order], tiled=True)


def leader(cols):
    return cols // 2


def other_core(value):
    return lax.ppermute(value, "core", [(0, 1), (1, 0)])


def left_parity(chip, col):
    home = col // 2
    return jnp.where(chip < home, col % 2, 1 - col % 2)


def rows_kernel(length, block, cols, act, grad, w_in, w_out, out, act_v, grad_v, in_v, out_v, w_sem, x_sem):
    seqs = out.shape[1]
    rank = w_in.shape[0]
    rows, width = act.shape
    steps = width // CHUNK
    sides = ((act, w_in, act_v, in_v), (grad, w_out, grad_v, out_v))
    copies = []
    for side, (x, w, x_v, w_v) in enumerate(sides):
        for step in range(steps):
            part = pl.ds(step * CHUNK, CHUNK)
            slot = side * steps + step
            pair = (
                pltpu.make_async_copy(w.at[:, part], w_v.at[:, part], w_sem.at[slot]),
                pltpu.make_async_copy(x.at[:, part], x_v.at[:, part], x_sem.at[slot]),
            )
            for copy in pair:
                copy.start()
            copies.append(pair)
    projected = []
    for side, (x, w, x_v, w_v) in enumerate(sides):
        total = jnp.zeros((rows, rank), jnp.float32)
        for step in range(steps):
            for copy in copies[side * steps + step]:
                copy.wait()
            part = pl.ds(step * CHUNK, CHUNK)
            total += lax.dot_general(
                x_v[:, part], w_v[:, part], NT, preferred_element_type=jnp.float32
            )
        projected.append(total)
    both = jnp.concatenate(projected, axis=1).T.astype(out.dtype)
    proj_act, proj_grad = both[:rank], both[rank:]
    many = rank // 2 * seqs
    row = lax.broadcasted_iota(jnp.int32, (many, rank), 0)
    column = lax.broadcasted_iota(jnp.int32, (many, rank), 1)
    token = lax.broadcasted_iota(jnp.int32, (many, rows), 1)
    sequence = lax.broadcasted_iota(jnp.int32, (many, rows), 0) % seqs
    left = []
    for odd in range(2):
        pick = (column == row // seqs * 2 + odd).astype(jnp.float32).astype(out.dtype)
        spread = jnp.dot(pick, proj_grad, preferred_element_type=jnp.float32)
        left.append(jnp.where(token // length == sequence, spread, 0.0).astype(out.dtype))
    nothing = jnp.zeros_like(proj_act)
    right = jnp.concatenate(
        [
            jnp.concatenate([proj_act, nothing], axis=1),
            jnp.concatenate([nothing, proj_act], axis=1),
        ]
    )
    summed = lax.dot_general(
        jnp.concatenate(left, axis=1), right, NT, preferred_element_type=jnp.float32
    )
    summed = summed * (1.0 / math.sqrt(length))
    lanes = 2 * rank
    tiles = block // lanes
    grad_rows = [
        summed[i * seqs : (i + 1) * seqs].astype(out.dtype) for i in range(many // seqs)
    ]
    for place in range(out.shape[0]):
        member = place ^ leader(cols)
        chip, col = member // cols, member % cols
        odd = col % 2 if chip < col // 2 else 1 - col % 2
        for slot, source in enumerate((2 * chip + odd, col)):
            for i in range(tiles):
                start = slot * block + i * lanes
                out[place, :, start : start + lanes] = grad_rows[source * tiles + i]


def gradient_pieces(plane, cols, block, activations, out_grads, w_in, w_out):
    seqs, length, width = activations.shape
    rank = w_in.shape[0]
    rows = seqs * length
    kind = activations.dtype
    steps = 2 * width // CHUNK
    return pl.pallas_call(
        functools.partial(rows_kernel, length, block, cols),
        out_shape=jax.ShapeDtypeStruct((plane, seqs, 2 * block), kind),
        in_specs=[HBM] * 4,
        out_specs=VMEM,
        scratch_shapes=[
            pltpu.VMEM((rows, width), kind),
            pltpu.VMEM((rows, width), kind),
            pltpu.VMEM((rank, width), kind),
            pltpu.VMEM((rank, width), kind),
            pltpu.SemaphoreType.DMA((steps,)),
            pltpu.SemaphoreType.DMA((steps,)),
        ],
        compiler_params=pltpu.CompilerParams(vmem_limit_bytes=LIMIT),
        cost_estimate=pl.CostEstimate(
            flops=4 * rows * width * rank, bytes_accessed=4 * (rows + rank) * width, transcendentals=0
        ),
        name="gradient_pieces",
    )(activations.reshape(rows, width), out_grads.reshape(rows, width), w_in, w_out)


def fetch_kernel(block, out, sem):
    copy = pltpu.make_async_copy(block, out, sem)
    copy.start()
    copy.wait()


def fetch(block):
    return pl.pallas_call(
        fetch_kernel,
        out_shape=jax.ShapeDtypeStruct(block.shape, block.dtype),
        in_specs=[HBM],
        out_specs=VMEM,
        scratch_shapes=[pltpu.SemaphoreType.DMA],
        compiler_params=pltpu.CompilerParams(vmem_limit_bytes=FETCH_LIMIT),
        cost_estimate=pl.CostEstimate(
            flops=0, bytes_accessed=2 * block.size * block.dtype.itemsize, transcendentals=0
        ),
        name="fetch",
    )(block)


def precond_kernel(case, got, own, other, out):
    block = own.shape[0]
    tile = min(256, block)
    half = block // 2
    left, right = got.at[:, :block], got.at[:, block:]

    def product(lhs, rhs):
        return jnp.dot(lhs, rhs, preferred_element_type=jnp.float32)

    def whole(pair):
        out[...] = product(left[...], pair[...]).astype(out.dtype)

    def at_home(odd, diagonal, pair):
        for start in range(0, block, tile):
            lanes = slice(start, start + tile)
            total = product(right[:, lanes] * 0.5, diagonal[lanes, lanes])
            if start > 0:
                total += product(right[:, :start], diagonal[:start, lanes])
            if not odd:
                total += product(left[:, :half], pair[:half, lanes])
            elif start + tile > half:
                skip = max(half - start, 0)
                more = product(left[...], pair[:, start + skip : start + tile])
                if skip > 0:
                    more = jnp.concatenate([jnp.zeros((left.shape[0], skip), jnp.float32), more], axis=1)
                total += more
            out[:, lanes] = total.astype(out.dtype)

    branches = [
        functools.partial(whole, own),
        functools.partial(whole, other),
        functools.partial(at_home, False, own, other),
        functools.partial(at_home, False, other, own),
        functools.partial(at_home, True, own, other),
        functools.partial(at_home, True, other, own),
    ]
    for i, branch in enumerate(branches):
        pl.when(case[0] == i)(branch)


def precondition(case, got, own, other):
    rows = got.shape[0]
    block, width = own.shape
    return pl.pallas_call(
        precond_kernel,
        out_shape=jax.ShapeDtypeStruct((rows, width), got.dtype),
        in_specs=[pl.BlockSpec(memory_space=pltpu.SMEM)] + [VMEM] * 3,
        out_specs=VMEM,
        compiler_params=pltpu.CompilerParams(vmem_limit_bytes=16 * 2**20),
        cost_estimate=pl.CostEstimate(
            flops=2 * rows * block * width, bytes_accessed=4 * block * width, transcendentals=0
        ),
        name="precondition",
    )(case, got, own, other)


def terms_kernel(n, fold, scale, core, precond, right, out):
    chips = n // 2
    size = right.shape[0] // n
    step = size // fold

    def packed(terms, row, col):
        lanes = terms[row * size : (row + 1) * size, col * size : (col + 1) * size]
        return jnp.concatenate([lanes[i * step : (i + 1) * step] for i in range(fold)], axis=1)

    def add(first, count):
        held = precond[pl.ds(first * size, count * size), :]
        once = lax.dot_general(held, right[...], NT, preferred_element_type=jnp.float32) * scale
        turned = lax.dot_general(right[...], held, NT, preferred_element_type=jnp.float32) * scale
        for chip in range(count):
            mine = 2 * (first + chip) + core[0]
            across = ((2 * (first + chip)) ^ (n // 2)) + core[0]
            for place in range(n):
                out[mine * n + (place ^ (n // 2))] += packed(once, chip, place)
                out[place * n + across] += packed(turned, place, chip)

    out[...] = jnp.zeros_like(out)
    if chips <= 2:
        add(0, chips)
    else:
        pl.loop(0, chips)(functools.partial(add, count=1))


def kernel_terms(n, fold, scale, core, precond, right):
    rows, width = precond.shape
    other = right.shape[0]
    size = other // n
    return pl.pallas_call(
        functools.partial(terms_kernel, n, fold, scale),
        out_shape=jax.ShapeDtypeStruct((n * n, size // fold, fold * size), jnp.float32),
        in_specs=[pl.BlockSpec(memory_space=pltpu.SMEM)] + [VMEM] * 2,
        out_specs=VMEM,
        compiler_params=pltpu.CompilerParams(
            vmem_limit_bytes=max(16 * 2**20, 12 * other * other)
        ),
        cost_estimate=pl.CostEstimate(
            flops=4 * rows * other * width, bytes_accessed=4 * other * other, transcendentals=0
        ),
        name="kernel_terms",
    )(core, precond, right)


def per_device(chips, cols, activations, out_grads, proj_in, proj_out, inv_gram):
    seqs, length, width = activations.shape
    rank = proj_in.shape[1]
    feat = rank * rank
    block = inv_gram.shape[0]
    plane = chips * cols
    half = seqs * plane
    tall = half // chips
    chip, core, col = (lax.axis_index(name) for name in ("chip", "core", "gc"))

    inv_other = other_core(inv_gram)

    pieces = gradient_pieces(plane, cols, block, activations, out_grads, proj_in.T, proj_out.T)
    pieces, inv_other = lax.optimization_barrier((pieces, inv_other))
    inv_other = fetch(inv_other)
    first = leader(cols)
    got = exchange(pieces, PLANE, plane, first)
    got = jnp.concatenate([got[i ^ first] for i in range(plane)])

    mine = got[:, block:]
    theirs = other_core(mine)
    home = col // 2 == chip
    left_other = (left_parity(chip, col) != core).astype(jnp.int32)
    diagonal_other = (col % 2 != core).astype(jnp.int32)
    case = jnp.where(home, 2 + 2 * (col % 2) + diagonal_other, left_other).astype(jnp.int32)
    theirs, precond = lax.optimization_barrier(
        (theirs, precondition(case.reshape(1), got, inv_gram, inv_other))
    )
    mine = mine.reshape(chips, 1, tall, block)
    theirs = theirs.reshape(chips, 1, tall, block)
    right = jnp.where(
        core == 0,
        jnp.concatenate([mine, theirs], axis=1),
        jnp.concatenate([theirs, mine], axis=1),
    ).reshape(2 * half, block)

    fold = max(1, 128 // tall)
    terms = kernel_terms(cols, fold, 8.0 / feat, core.reshape(1).astype(jnp.int32), precond, right)
    total = jnp.sum(exchange(terms, ("chip", "core", "gc"), cols * cols, cols // 2), axis=0)
    return jnp.concatenate([total[:, i * tall : (i + 1) * tall] for i in range(fold)])


def solution(mesh):
    grp, gr, gc = (mesh.shape[name] for name in ("grp", "gr", "gc"))
    split = Mesh(mesh.devices.reshape(grp, gr // 2, 2, gc), ("grp", "chip", "core", "gc"))
    rows = ("grp", "chip", "core", "gc")
    in_specs = (P(rows, None, None), P(rows, None, None), P(), P(), P(("chip", "core"), "gc"))
    out_specs = P(("grp", "chip", "core"), "gc")

    def fn(*args):
        return per_device(gr // 2, gc, *args)

    return jax.shard_map(fn, mesh=split, in_specs=in_specs, out_specs=out_specs, check_vma=False)
```

```python
import functools
import math

import jax
import jax.numpy as jnp
from jax import lax
from jax.experimental import pallas as pl
from jax.experimental.pallas import tpu as pltpu
from jax.sharding import Mesh, PartitionSpec as P

PLANE = ("chip", "gc")
CHUNK = 512
FETCH_LIMIT = 16 * 2**20
LIMIT = 107 * 2**19
VMEM = pl.BlockSpec(memory_space=pltpu.VMEM)
HBM = pl.BlockSpec(memory_space=pl.ANY)
NT = (((1,), (1,)), ((), ()))


def exchange(value, axes, members, first):
    order = [i ^ first for i in range(members)]
    return lax.all_to_all(value, axes, 0, 0, axis_index_groups=[order], tiled=True)


def leader(chips, cols):
    return chips // 2 * cols + cols // 2


def other_core(value):
    return lax.ppermute(value, "core", [(0, 1), (1, 0)])


def left_parity(chip, col):
    home = col // 2
    return jnp.where(chip < home, col % 2, 1 - col % 2)


def rows_kernel(length, block, cols, act, grad, w_in, w_out, out, act_v, grad_v, in_v, out_v, w_sem, x_sem):
    seqs = out.shape[1]
    rank = w_in.shape[0]
    rows, width = act.shape
    steps = width // CHUNK
    sides = ((act, w_in, act_v, in_v), (grad, w_out, grad_v, out_v))
    copies = []
    for side, (x, w, x_v, w_v) in enumerate(sides):
        for step in range(steps):
            part = pl.ds(step * CHUNK, CHUNK)
            slot = side * steps + step
            pair = (
                pltpu.make_async_copy(w.at[:, part], w_v.at[:, part], w_sem.at[slot]),
                pltpu.make_async_copy(x.at[:, part], x_v.at[:, part], x_sem.at[slot]),
            )
            for copy in pair:
                copy.start()
            copies.append(pair)
    projected = []
    for side, (x, w, x_v, w_v) in enumerate(sides):
        total = jnp.zeros((rows, rank), jnp.float32)
        for step in range(steps):
            for copy in copies[side * steps + step]:
                copy.wait()
            part = pl.ds(step * CHUNK, CHUNK)
            total += lax.dot_general(
                x_v[:, part], w_v[:, part], NT, preferred_element_type=jnp.float32
            )
        projected.append(total)
    both = jnp.concatenate(projected, axis=1).T.astype(out.dtype)
    proj_act, proj_grad = both[:rank], both[rank:]
    many = rank // 2 * seqs
    row = lax.broadcasted_iota(jnp.int32, (many, rank), 0)
    column = lax.broadcasted_iota(jnp.int32, (many, rank), 1)
    token = lax.broadcasted_iota(jnp.int32, (many, rows), 1)
    sequence = lax.broadcasted_iota(jnp.int32, (many, rows), 0) % seqs
    left = []
    for odd in range(2):
        pick = (column == row // seqs * 2 + odd).astype(jnp.float32).astype(out.dtype)
        spread = jnp.dot(pick, proj_grad, preferred_element_type=jnp.float32)
        left.append(jnp.where(token // length == sequence, spread, 0.0).astype(out.dtype))
    nothing = jnp.zeros_like(proj_act)
    right = jnp.concatenate(
        [
            jnp.concatenate([proj_act, nothing], axis=1),
            jnp.concatenate([nothing, proj_act], axis=1),
        ]
    )
    summed = lax.dot_general(
        jnp.concatenate(left, axis=1), right, NT, preferred_element_type=jnp.float32
    )
    summed = summed * (1.0 / math.sqrt(length))
    lanes = 2 * rank
    tiles = block // lanes
    grad_rows = [
        summed[i * seqs : (i + 1) * seqs].astype(out.dtype) for i in range(many // seqs)
    ]
    for place in range(out.shape[0]):
        member = place ^ leader(out.shape[0] // cols, cols)
        chip, col = member // cols, member % cols
        odd = col % 2 if chip < col // 2 else 1 - col % 2
        for slot, source in enumerate((2 * chip + odd, col)):
            for i in range(tiles):
                start = slot * block + i * lanes
                out[place, :, start : start + lanes] = grad_rows[source * tiles + i]


def gradient_pieces(plane, cols, block, activations, out_grads, w_in, w_out):
    seqs, length, width = activations.shape
    rank = w_in.shape[0]
    rows = seqs * length
    kind = activations.dtype
    steps = 2 * width // CHUNK
    return pl.pallas_call(
        functools.partial(rows_kernel, length, block, cols),
        out_shape=jax.ShapeDtypeStruct((plane, seqs, 2 * block), kind),
        in_specs=[HBM] * 4,
        out_specs=VMEM,
        scratch_shapes=[
            pltpu.VMEM((rows, width), kind),
            pltpu.VMEM((rows, width), kind),
            pltpu.VMEM((rank, width), kind),
            pltpu.VMEM((rank, width), kind),
            pltpu.SemaphoreType.DMA((steps,)),
            pltpu.SemaphoreType.DMA((steps,)),
        ],
        compiler_params=pltpu.CompilerParams(vmem_limit_bytes=LIMIT),
        cost_estimate=pl.CostEstimate(
            flops=4 * rows * width * rank, bytes_accessed=4 * (rows + rank) * width, transcendentals=0
        ),
        name="gradient_pieces",
    )(activations.reshape(rows, width), out_grads.reshape(rows, width), w_in, w_out)


def fetch_kernel(block, out, sem):
    copy = pltpu.make_async_copy(block, out, sem)
    copy.start()
    copy.wait()


def fetch(block):
    return pl.pallas_call(
        fetch_kernel,
        out_shape=jax.ShapeDtypeStruct(block.shape, block.dtype),
        in_specs=[HBM],
        out_specs=VMEM,
        scratch_shapes=[pltpu.SemaphoreType.DMA],
        compiler_params=pltpu.CompilerParams(vmem_limit_bytes=FETCH_LIMIT),
        cost_estimate=pl.CostEstimate(
            flops=0, bytes_accessed=2 * block.size * block.dtype.itemsize, transcendentals=0
        ),
        name="fetch",
    )(block)


def precond_kernel(case, got, own, other, out):
    block = own.shape[0]
    tile = min(256, block)
    half = block // 2
    left, right = got.at[:, :block], got.at[:, block:]

    def product(lhs, rhs):
        return jnp.dot(lhs, rhs, preferred_element_type=jnp.float32)

    def whole(pair):
        out[...] = product(left[...], pair[...]).astype(out.dtype)

    def at_home(odd, diagonal, pair):
        for start in range(0, block, tile):
            lanes = slice(start, start + tile)
            total = product(right[:, lanes] * 0.5, diagonal[lanes, lanes])
            if start > 0:
                total += product(right[:, :start], diagonal[:start, lanes])
            if not odd:
                total += product(left[:, :half], pair[:half, lanes])
            elif start + tile > half:
                skip = max(half - start, 0)
                more = product(left[...], pair[:, start + skip : start + tile])
                if skip > 0:
                    more = jnp.concatenate([jnp.zeros((left.shape[0], skip), jnp.float32), more], axis=1)
                total += more
            out[:, lanes] = total.astype(out.dtype)

    branches = [
        functools.partial(whole, own),
        functools.partial(whole, other),
        functools.partial(at_home, False, own, other),
        functools.partial(at_home, False, other, own),
        functools.partial(at_home, True, own, other),
        functools.partial(at_home, True, other, own),
    ]
    for i, branch in enumerate(branches):
        pl.when(case[0] == i)(branch)


def precondition(case, got, own, other):
    rows = got.shape[0]
    block, width = own.shape
    return pl.pallas_call(
        precond_kernel,
        out_shape=jax.ShapeDtypeStruct((rows, width), got.dtype),
        in_specs=[pl.BlockSpec(memory_space=pltpu.SMEM)] + [VMEM] * 3,
        out_specs=VMEM,
        compiler_params=pltpu.CompilerParams(vmem_limit_bytes=16 * 2**20),
        cost_estimate=pl.CostEstimate(
            flops=2 * rows * block * width, bytes_accessed=4 * block * width, transcendentals=0
        ),
        name="precondition",
    )(case, got, own, other)


def terms_kernel(n, fold, scale, core, precond, right, out):
    chips = n // 2
    size = right.shape[0] // n
    step = size // fold

    def packed(terms, row, col):
        lanes = terms[row * size : (row + 1) * size, col * size : (col + 1) * size]
        return jnp.concatenate([lanes[i * step : (i + 1) * step] for i in range(fold)], axis=1)

    def add(first, count):
        held = precond[pl.ds(first * size, count * size), :]
        once = lax.dot_general(held, right[...], NT, preferred_element_type=jnp.float32) * scale
        turned = lax.dot_general(right[...], held, NT, preferred_element_type=jnp.float32) * scale
        for chip in range(count):
            mine = 2 * (first + chip) + core[0]
            across = ((2 * (first + chip)) ^ (n // 2)) + core[0]
            for place in range(n):
                out[mine * n + (place ^ (n // 2))] += packed(once, chip, place)
                out[place * n + across] += packed(turned, place, chip)

    out[...] = jnp.zeros_like(out)
    if chips <= 2:
        add(0, chips)
    else:
        pl.loop(0, chips)(functools.partial(add, count=1))


def kernel_terms(n, fold, scale, core, precond, right):
    rows, width = precond.shape
    other = right.shape[0]
    size = other // n
    return pl.pallas_call(
        functools.partial(terms_kernel, n, fold, scale),
        out_shape=jax.ShapeDtypeStruct((n * n, size // fold, fold * size), jnp.float32),
        in_specs=[pl.BlockSpec(memory_space=pltpu.SMEM)] + [VMEM] * 2,
        out_specs=VMEM,
        compiler_params=pltpu.CompilerParams(
            vmem_limit_bytes=max(16 * 2**20, 12 * other * other)
        ),
        cost_estimate=pl.CostEstimate(
            flops=4 * rows * other * width, bytes_accessed=4 * other * other, transcendentals=0
        ),
        name="kernel_terms",
    )(core, precond, right)


def per_device(chips, cols, activations, out_grads, proj_in, proj_out, inv_gram):
    seqs, length, width = activations.shape
    rank = proj_in.shape[1]
    feat = rank * rank
    block = inv_gram.shape[0]
    plane = chips * cols
    half = seqs * plane
    tall = half // chips
    chip, core, col = (lax.axis_index(name) for name in ("chip", "core", "gc"))

    inv_other = other_core(inv_gram)

    pieces = gradient_pieces(plane, cols, block, activations, out_grads, proj_in.T, proj_out.T)
    pieces, inv_other = lax.optimization_barrier((pieces, inv_other))
    inv_other = fetch(inv_other)
    first = leader(chips, cols)
    got = exchange(pieces, PLANE, plane, first)
    got = jnp.concatenate([got[i ^ first] for i in range(plane)])

    mine = got[:, block:]
    theirs = other_core(mine)
    home = col // 2 == chip
    left_other = (left_parity(chip, col) != core).astype(jnp.int32)
    diagonal_other = (col % 2 != core).astype(jnp.int32)
    case = jnp.where(home, 2 + 2 * (col % 2) + diagonal_other, left_other).astype(jnp.int32)
    theirs, precond = lax.optimization_barrier(
        (theirs, precondition(case.reshape(1), got, inv_gram, inv_other))
    )
    mine = mine.reshape(chips, 1, tall, block)
    theirs = theirs.reshape(chips, 1, tall, block)
    right = jnp.where(
        core == 0,
        jnp.concatenate([mine, theirs], axis=1),
        jnp.concatenate([theirs, mine], axis=1),
    ).reshape(2 * half, block)

    fold = max(1, 128 // tall)
    terms = kernel_terms(cols, fold, 8.0 / feat, core.reshape(1).astype(jnp.int32), precond, right)
    total = jnp.sum(exchange(terms, ("chip", "core", "gc"), cols * cols, cols // 2), axis=0)
    return jnp.concatenate([total[:, i * tall : (i + 1) * tall] for i in range(fold)])


def solution(mesh):
    grp, gr, gc = (mesh.shape[name] for name in ("grp", "gr", "gc"))
    split = Mesh(mesh.devices.reshape(grp, gr // 2, 2, gc), ("grp", "chip", "core", "gc"))
    rows = ("grp", "chip", "core", "gc")
    in_specs = (P(rows, None, None), P(rows, None, None), P(), P(), P(("chip", "core"), "gc"))
    out_specs = P(("grp", "chip", "core"), "gc")

    def fn(*args):
        return per_device(gr // 2, gc, *args)

    return jax.shard_map(fn, mesh=split, in_specs=in_specs, out_specs=out_specs, check_vma=False)
```
